512 devices in a mesh: pair: 2 (over core), dp: 16 (over x, z_lo), fsdp: 16 (over y, z_hi).
Axes of the slice: x: 4, y: 4, z: 16 (z_hi: 4, z_lo: 4; z = z_hi * 4 + z_lo), core: 2. Of those that a mesh axis runs over, the one named last changes fastest.
Arguments:
- features: bfloat16 [2, 320, 262144], P('pair', None, ('dp', 'fsdp')), may hold values from -6 to 6
- level_gain: float32 [64, 320], replicated, may hold values from 0.5 to 1.5
- levels: int32 [64], replicated, may hold values from 0 to 63
- w_in: bfloat16 [2, 1280, 320], P('pair', 'fsdp'), may hold values from -0.3125 to 0.3125
- w_down: bfloat16 [2, 1280, 320], P('pair', 'fsdp'), may hold values from -0.15625 to 0.15625
- w_rgb: float32 [2, 3, 320], P('pair'), may hold values from -0.3125 to 0.3125
- target: float32 [3, 262144], P(None, ('dp', 'fsdp')), may hold values from -6 to 6
- counts: int32 [262144], P(('dp', 'fsdp')), may hold values from 1 to 1024
Outputs:
- predictions: float32 [2, 3, 262144], P('pair', None, ('dp', 'fsdp'))
- grad_in: float32 [2, 1280, 320], P('pair', 'fsdp')
- grad_down: float32 [2, 1280, 320], P('pair', 'fsdp')
The draws below stay inside these ranges and needn't reach their ends.
All inputs are finite; a program needn't handle non-finite values.
Results may differ from the reference program's by a relative error of at most 0.0022.
Values may be sent and summed in bfloat16 or wider, within the bound.
A program may use at most 64 MiB of HBM per device.

```python
import math
import jax
import jax.numpy as jnp
from jax import lax

C = 320
H = 1280
LEVELS = 64
IMG_PIX = 4096
PIXELS = 262144
IMAGES = 64


def set_ends(result, stream_key, low, top_value):
    shape = result.shape
    spot = [jax.random.randint(jax.random.fold_in(stream_key, axis), (), 0, shape[axis]) for axis in range(len(shape))]
    result = result.at[tuple(spot)].set(low)
    longest = shape.index(max(shape))
    spot[longest] = (spot[longest] + 1) % shape[longest]
    return result.at[tuple(spot)].set(top_value)


def shard_levels(key, shape, cuts, low, largest):
    def one(position, shards_of):
        draws = jax.random.uniform(jax.random.fold_in(jax.random.fold_in(key, 6), position), (shards_of,), jnp.float32, low / len(cuts), largest / len(cuts))
        return jnp.repeat(jnp.exp(draws), shape[position] // shards_of).reshape((-1,) + (1,) * (len(shape) - position - 1))

    level = one(*cuts[0])
    for cut in cuts[1:]:
        level = level * one(*cut)
    return level


def normal_values(own_key, dims, spread, limit, shards=(), held_as=jnp.bfloat16):
    level = shard_levels(own_key, dims, shards, -0.22, 0.18) if shards else 1.0
    result = jax.random.normal(own_key, dims, jnp.float32) * spread * level
    return jnp.minimum(jnp.maximum(result, -limit), limit).astype(held_as)


def setup_inputs(seed: int = 0) -> dict:
    streams_of = jax.random.split(jax.random.key(seed), 9)
    return {
        "features": normal_values(streams_of[0], (2, C, PIXELS), 1.0, 6.0, ((0, 2), (2, 256))),
        "level_gain": jnp.clip(jax.random.uniform(streams_of[1], (LEVELS, C), jnp.float32, 0.5, 1.5), 0.5, 1.5),
        "levels": set_ends(jax.random.randint(streams_of[2], (IMAGES,), 0, LEVELS), jax.random.fold_in(streams_of[2], 1), 0, LEVELS - 1).astype(jnp.int32),
        "w_in": normal_values(streams_of[3], (2, H, C), C ** -0.5, 0.3125, ((0, 2), (1, 16))),
        "w_down": normal_values(streams_of[4], (2, H, C), H ** -0.5, 0.15625, ((0, 2), (1, 16))),
        "w_rgb": normal_values(streams_of[5], (2, 3, C), C ** -0.5, 0.3125, ((0, 2),), jnp.float32),
        "target": normal_values(streams_of[6], (3, PIXELS), 1.0, 6.0, ((1, 256),), jnp.float32),
        "counts": set_ends(jax.random.randint(streams_of[7], (PIXELS,), 1, 1025), jax.random.fold_in(streams_of[7], 1), 1, 1024).astype(jnp.int32),
    }


EPS = 1e-06
DISTILL = 1.0

def forward(x, gain, w_in, w_down, w_rgb):
    xf = x.astype(jnp.float32)
    mean_sq = lax.optimization_barrier(jnp.mean(xf * xf, axis=0, keepdims=True))
    normed = (xf * lax.rsqrt(mean_sq + EPS) * gain[:, None]).astype(jnp.bfloat16)
    pre = jnp.dot(w_in, normed, preferred_element_type=jnp.float32)
    hidden = jax.nn.silu(pre).astype(jnp.bfloat16)
    delta = lax.dot_general(w_down, hidden, (((0,), (0,)), ((), ())), preferred_element_type=jnp.float32)
    mixed = xf + delta
    pred = jnp.dot(w_rgb, mixed, precision=lax.Precision.HIGHEST)
    return (normed, pre, hidden, pred)

def reference(features, level_gain, levels, w_in, w_down, w_rgb, target, counts):
    pixels_all = features.shape[2]
    images = pixels_all // IMG_PIX
    loss_scale = math.sqrt(C / pixels_all)
    blocks = jnp.arange(images, dtype=jnp.int32)

    def preds_of(replica):

        def one(index):
            start = (index * IMG_PIX).astype(jnp.int32)
            x = lax.dynamic_slice_in_dim(features[replica], start, IMG_PIX, 1)
            gain = level_gain[levels[index]]
            return forward(x, gain, w_in[replica], w_down[replica], w_rgb[replica])[3]
        stacked = lax.map(one, blocks)
        return jnp.transpose(stacked, (1, 0, 2)).reshape(3, pixels_all)
    preds = jnp.stack([preds_of(0), preds_of(1)])

    def grads_of(replica):

        def step(carry, index):
            start = (index * IMG_PIX).astype(jnp.int32)
            x = lax.dynamic_slice_in_dim(features[replica], start, IMG_PIX, 1)
            gain = level_gain[levels[index]]
            normed, pre, hidden, pred = forward(x, gain, w_in[replica], w_down[replica], w_rgb[replica])
            goal = lax.dynamic_slice_in_dim(target, start, IMG_PIX, 1)
            partner = lax.dynamic_slice_in_dim(preds[1 - replica], start, IMG_PIX, 1)
            samples = lax.dynamic_slice_in_dim(counts, start, IMG_PIX, 0).astype(jnp.float32)
            weight = samples / (samples + 64.0)
            g_pred = (weight * (pred - goal) + DISTILL * (pred - partner)) * loss_scale
            g_mixed = jnp.dot(w_rgb[replica].T, g_pred, precision=lax.Precision.HIGHEST).astype(jnp.bfloat16)
            g_hidden = jnp.dot(w_down[replica], g_mixed, preferred_element_type=jnp.float32)
            sig = jax.nn.sigmoid(pre)
            g_pre = (g_hidden * sig * (1.0 + pre * (1.0 - sig))).astype(jnp.bfloat16)
            grad_one = lax.dot_general(g_pre, normed, (((1,), (1,)), ((), ())), preferred_element_type=jnp.float32)
            grad_two = lax.dot_general(hidden, g_mixed, (((1,), (1,)), ((), ())), preferred_element_type=jnp.float32)
            return ((carry[0] + grad_one, carry[1] + grad_two), None)
        empty = jnp.zeros(w_in.shape[1:], jnp.float32)
        totals, unused = lax.scan(step, (empty, empty), blocks)
        return totals
    first = grads_of(0)
    second = grads_of(1)
    return (preds, jnp.stack([first[0], second[0]]), jnp.stack([first[1], second[1]]))
```

```python
import math

import jax
import jax.numpy as jnp
from jax import lax
from jax.sharding import PartitionSpec as P

IMG_PIX = 4096


EPS = 1e-06
DISTILL = 1.0


def from_partner(value, axis, apart):
    return lax.ppermute(value, axis, [(i, i ^ 1 << apart) for i in range(lax.axis_size(axis))])


def contract_rows(left, right):
    return lax.dot_general(
        left, right, (((1,), (1,)), ((), ())), preferred_element_type=jnp.float32
    )


def on_device(features, level_gain, levels, w_in, w_down, w_rgb, target, counts):
    x_local = features[0]
    pixels = x_local.shape[1]
    offset = lax.axis_index(("dp", "fsdp")) * pixels
    image = offset // IMG_PIX
    level = jnp.sum(jnp.where(jnp.arange(levels.shape[0], dtype=jnp.int32) == image, levels, 0))
    table_rows = jnp.arange(level_gain.shape[0], dtype=jnp.int32)[:, None]
    gain = jnp.sum(jnp.where(table_rows == level, level_gain, 0.0), axis=0)
    xf = x_local.astype(jnp.float32)
    mean_sq = jnp.mean(xf * xf, axis=0, keepdims=True)
    normed = (xf * lax.rsqrt(mean_sq + EPS) * gain[:, None]).astype(jnp.bfloat16)
    high = lax.Precision.HIGHEST
    head_rows = lax.dot_general(
        w_down[0].astype(jnp.float32), w_rgb[0], (((1,), (1,)), ((), ())), precision=high
    )
    head = lax.all_gather(head_rows, "fsdp", axis=0, tiled=True)
    pre = jnp.dot(
        lax.all_gather(w_in[0], "fsdp", axis=0, tiled=True),
        normed,
        preferred_element_type=jnp.float32,
    )
    sig = jax.nn.sigmoid(pre)
    hidden = (pre * sig).astype(jnp.bfloat16)
    pred = jnp.dot(w_rgb[0], xf, precision=high) + jnp.dot(
        head.T, hidden.astype(jnp.float32), precision=high
    )
    partner = from_partner(pred, "pair", 0)
    pixels_all = pixels * lax.axis_size("dp") * lax.axis_size("fsdp")
    loss_scale = math.sqrt(xf.shape[0] / pixels_all)
    samples = counts.astype(jnp.float32)
    weight = samples / (samples + 64.0)
    g_pred = (weight * (pred - target) + DISTILL * (pred - partner)) * loss_scale
    g_hidden = jnp.dot(head, g_pred, precision=high)
    g_pre = (g_hidden * sig * (1.0 + pre * (1.0 - sig))).astype(jnp.bfloat16)
    channels = normed.shape[0]
    grad_head = lax.dot_general(
        hidden.astype(jnp.float32), g_pred, (((1,), (1,)), ((), ())), precision=high
    )
    partial_rows = lax.psum_scatter(
        jnp.concatenate([contract_rows(g_pre, normed), grad_head], axis=1),
        "fsdp",
        scatter_dimension=0,
        tiled=True,
    )
    totals = lax.psum(partial_rows, "dp")
    grad_down = jnp.dot(totals[:, channels:], w_rgb[0], precision=high)
    return (pred[None], totals[:, :channels][None], grad_down[None])


def solution(mesh):
    in_specs = (
        P("pair", None, ("dp", "fsdp")),
        P(),
        P(),
        P("pair", "fsdp", None),
        P("pair", "fsdp", None),
        P("pair", None, None),
        P(None, ("dp", "fsdp")),
        P(("dp", "fsdp")),
    )
    out_specs = (P("pair", None, ("dp", "fsdp")), P("pair", "fsdp", None), P("pair", "fsdp", None))
    return jax.shard_map(
        on_device, mesh=mesh, in_specs=in_specs, out_specs=out_specs, check_vma=False
    )
```

```python
import math

import jax
import jax.numpy as jnp
from jax import lax
from jax.experimental import pallas as pl
from jax.experimental.pallas import tpu as pltpu
from jax.sharding import PartitionSpec as P

IMG_PIX = 4096
EPS = 1e-06
DISTILL = 1.0

MESH = pl.DeviceIdType.MESH
HIGH = lax.Precision.HIGHEST
BF16 = jnp.bfloat16
F32 = jnp.float32

SIDE = 4
OTHERS = SIDE * SIDE - 1
TILE = (16, 128)
BANDS = 5
SLABS = 3
HEAD = 64


def dot(left, right, dims, **kw):
    return lax.dot_general(left, right, (dims, ((), ())), preferred_element_type=F32, **kw)


def kernel(
    loss_scale,
    x_ref, table_ref, levels_ref, w_in_ref, w_down_ref, w_rgb_ref, target_ref, counts_ref,
    pred_ref, grad_in_ref, grad_down_ref,
    rgb, normed, wbuf, wmat, hidden, slope, pred_mine, pred_other, g_rows, g_aug,
    gsend, grecv, zsend, zrecv, fbuf,
    a_send, a_recv, y_send, y_recv, b_send, b_recv, p_send, p_recv,
    r_send, r_recv, z_send, z_recv, f_send, f_recv,
):
    pair = lax.axis_index("pair")
    dp = lax.axis_index("dp")
    fsdp = lax.axis_index("fsdp")
    x, zl = dp // SIDE, dp % SIDE
    y, zh = fsdp // SIDE, fsdp % SIDE
    here = y * SIDE + x
    pixels = x_ref.shape[1]
    channels = x_ref.shape[0]
    rows = w_in_ref.shape[0]

    def device(x_, y_, zh_, zl_):
        return (pair, x_ * SIDE + zl_, y_ * SIDE + zh_)

    def plane_peer(i):
        return device((x + i % SIDE) % SIDE, (y + i // SIDE) % SIDE, zh, zl)

    def z_peer(i):
        return device(x, y, (zh + i // SIDE) % SIDE, (zl + i % SIDE) % SIDE)

    def dp_peer(i):
        return device((x + i // SIDE) % SIDE, y, zh, (zl + i % SIDE) % SIDE)

    barrier = pltpu.get_barrier_semaphore()

    def greet(peer):
        pl.semaphore_signal(barrier, inc=1, device_id=peer, device_id_type=MESH)

    def greet_all(i, carry):
        greet(plane_peer(i))
        greet(z_peer(i))
        return carry

    lax.fori_loop(1, OTHERS + 1, greet_all, 0)
    for a in range(1, SIDE):
        for b in range(1, SIDE):
            greet(dp_peer(a * SIDE + b))
    greet((1 - pair, dp, fsdp))

    rgb[...] = jnp.zeros_like(rgb)
    for copy in range(3):
        rgb[HEAD + 3 * copy : HEAD + 3 * copy + 3, :] = w_rgb_ref[...]
    lane = lax.broadcasted_iota(jnp.int32, (rows, 128), 1)
    head = dot(w_down_ref[...].astype(F32), rgb[...], ((1,), (1,)), precision=HIGH)
    head_hi = head.astype(BF16).astype(F32)
    is_lo = (lane >= HEAD + 3) & (lane < HEAD + 6)
    head = jnp.where(is_lo, head - head_hi, head_hi)
    w_own = w_in_ref[...]
    last = w_own[:, 256:320].astype(F32)
    last = jnp.concatenate([last, jnp.zeros((rows, 64), F32)], axis=1) + head
    slabs = [w_own[:, 0:128], w_own[:, 128:256], last.astype(BF16)]
    own_quarters = wbuf.at[zh]
    for band in range(BANDS):
        for slab in range(SLABS):
            q = band * SLABS + slab
            own_quarters[y * SIDE + q // SIDE, q % SIDE] = slabs[slab][16 * band : 16 * band + 16, :]
    own_quarters[y * SIDE + SIDE - 1, SIDE - 1] = jnp.zeros(TILE, BF16)

    pl.semaphore_wait(barrier, 2 * OTHERS + 9 + 1)

    def remote(src, dst, send, recv, peer):
        return pltpu.make_async_remote_copy(
            src_ref=src, dst_ref=dst, send_sem=send, recv_sem=recv,
            device_id=peer, device_id_type=MESH,
        )

    def wait_bytes(ref, sem):
        pltpu.make_async_copy(ref, ref, sem).wait()

    far_first = (2, 1, 3)
    quarter = wbuf.at[zh, here]
    along_z = {}
    for k in far_first:
        along_z[k] = remote(quarter, quarter, a_send.at[k], a_recv.at[k], device(x, y, (zh + k) % SIDE, zl))
        along_z[k].start()
    block = wbuf.at[zh, pl.ds(y * SIDE, SIDE)]
    along_y = []
    for m in range(1, SIDE):
        c = remote(block, block, y_send.at[m], y_recv.at[m], device(x, (y + m) % SIDE, zh, zl))
        c.start()
        along_y.append(c)

    image = ((dp * SIDE * SIDE + fsdp) * pixels) // IMG_PIX
    levels = levels_ref[...].astype(F32)
    spots = lax.broadcasted_iota(jnp.int32, levels.shape, 1)
    level = jnp.sum(jnp.where(spots == image, levels, 0.0), axis=1, keepdims=True)
    table_rows = lax.broadcasted_iota(jnp.int32, table_ref.shape, 0).astype(F32)
    gain = jnp.sum(jnp.where(table_rows == level, table_ref[...], 0.0), axis=0, keepdims=True)
    gain = jnp.concatenate([gain, jnp.zeros((1, 384 - channels), F32)], axis=1)
    gain = jnp.broadcast_to(gain, (128, 384)).T[:channels, 0:1]
    xf = x_ref[...].astype(F32)
    mean_sq = jnp.mean(xf * xf, axis=0, keepdims=True)
    normed[0:channels, :] = (xf * lax.rsqrt(mean_sq + EPS) * gain).astype(BF16)
    normed[channels:, :] = jnp.zeros((384 - channels, pixels), BF16)

    part = rgb[HEAD : HEAD + 16, :]
    part_hi = part.astype(BF16).astype(F32)
    part_mid = (part - part_hi).astype(BF16).astype(F32)
    part_lo = part - part_hi - part_mid
    row = lax.broadcasted_iota(jnp.int32, part.shape, 0)
    part = jnp.where(row < 3, part_hi, jnp.where(row < 6, part_mid, part_lo)).astype(BF16)
    direct = dot(part, x_ref[...], ((1,), (0,)))
    pred_mine[...] = jnp.zeros_like(pred_mine)
    pred_mine[0:3, :] = direct[0:3] + direct[3:6] + direct[6:9]

    wide = 256

    def forward(group):
        def assemble(yy, carry):
            for band in range(BANDS):
                for slab in range(SLABS):
                    q = band * SLABS + slab
                    wmat[group, pl.ds(yy * rows + 16 * band, 16), 128 * slab : 128 * slab + 128] = (
                        wbuf[group, yy * SIDE + q // SIDE, q % SIDE]
                    )
            return carry

        lax.fori_loop(0, SIDE, assemble, 0)

        def columns(n, carry):
            at = pl.ds(pl.multiple_of(n * wide, wide), wide)
            pre = dot(wmat[group], normed[:, at], ((1,), (0,)))
            sig = jax.nn.sigmoid(pre)
            hid = (pre * sig).astype(BF16)
            hidden[group, :, at] = hid
            slope[group, :, at] = sig * (1.0 + pre * (1.0 - sig))
            through = dot(wmat[group, :, 256:384], hid, ((0,), (0,)))
            pred_mine[0:3, at] += through[HEAD : HEAD + 3] + through[HEAD + 3 : HEAD + 6]
            return carry

        lax.fori_loop(0, pixels // wide, columns, 0)

    def forward_on(k):
        group = (zh + SIDE - k) % SIDE
        along_z[k].wait_recv()
        chunk = wbuf.at[group, here]

        def send(i, carry):
            remote(chunk, chunk, b_send.at[k], b_recv.at[k], plane_peer(i)).start()
            return carry

        lax.fori_loop(1, OTHERS + 1, send, 0)

    for c in along_y:
        c.wait_recv()
    for k in (1, 3, 2):
        forward_on(k)
    forward(zh)
    for k in (1, 3, 2):
        wait_bytes(wbuf.at[0, 0:OTHERS], b_recv.at[k])
        forward((zh + SIDE - k) % SIDE)

    swap = remote(pred_mine, pred_other, p_send, p_recv, (1 - pair, dp, fsdp))
    swap.start()
    pred = pred_mine[0:3, :]
    pred_ref[...] = pred
    samples = counts_ref[...].astype(F32)
    weight = samples / (samples + 64.0)
    toward = weight * (pred - target_ref[...])
    swap.wait_recv()
    g_pred = (toward + DISTILL * (pred - pred_other[0:3, :])) * loss_scale
    g_hi = g_pred.astype(BF16).astype(F32)
    g_rows[...] = jnp.zeros_like(g_rows)
    g_rows[0:3, :] = g_hi
    g_rows[3:6, :] = g_hi
    g_rows[6:9, :] = g_pred - g_hi
    g_aug[...] = jnp.zeros_like(g_aug)
    g_aug[HEAD : HEAD + 16, :] = g_rows[...].astype(BF16)

    lane_g = lax.broadcasted_iota(jnp.int32, (SIDE * rows, 128), 1)
    is_rest = (lane_g >= HEAD + 3) & (lane_g < HEAD + 6)

    def backward(group):
        g_hidden = dot(wmat[group, :, 256:384], g_aug[...], ((1,), (0,)))
        g_pre = (g_hidden * slope[group]).astype(BF16)
        grad = dot(g_pre, normed[...], ((1,), (1,)))
        for_head = dot(hidden[group], g_aug[...], ((1,), (1,)))
        for_head = jnp.where(is_rest, for_head - for_head.astype(BF16).astype(F32), for_head)
        out = [
            grad[:, 0:128].astype(BF16),
            grad[:, 128:256].astype(BF16),
            (grad[:, 256:384] + for_head).astype(BF16),
        ]
        for yy in range(SIDE):
            for band in range(BANDS):
                for slab in range(SLABS):
                    q = band * SLABS + slab
                    top = yy * rows + 16 * band
                    gsend[group, yy * SIDE + q // SIDE, q % SIDE] = out[slab][top : top + 16, :]
            gsend[group, yy * SIDE + SIDE - 1, SIDE - 1] = jnp.zeros(TILE, BF16)

        def send(i, carry):
            there = ((y + i // SIDE) % SIDE) * SIDE + (x + i % SIDE) % SIDE
            remote(
                gsend.at[group, there], grecv.at[group, here],
                r_send.at[group], r_recv.at[group], plane_peer(i),
            ).start()
            return carry

        lax.fori_loop(1, OTHERS + 1, send, 0)
        grecv[group, here] = gsend[group, here]

    order = [(zh + k) % SIDE for k in (2, 1, 3, 0)]

    def plane_sum(k, group):
        wait_bytes(grecv.at[0, 0:OTHERS], r_recv.at[group])
        total = grecv[group, 0].astype(F32)
        for s in range(1, SIDE * SIDE):
            total = total + grecv[group, s].astype(F32)
        zsend[group] = total

        def send(b, carry):
            to = (zl + b) % SIDE
            remote(
                zsend.at[group, to], zrecv.at[zh * SIDE + zl], z_send, z_recv, device(x, y, group, to)
            ).start()
            return carry

        lax.fori_loop(1 if k == 0 else 0, SIDE, send, 0)

    for group in order:
        backward(group)
    for k, group in zip((2, 1, 3, 0), order):
        plane_sum(k, group)
    zrecv[zh * SIDE + zl] = zsend[zh, zl]
    wait_bytes(zrecv.at[0:OTHERS], z_recv)
    total = zrecv[0]
    for s in range(1, SIDE * SIDE):
        total = total + zrecv[s]
    own = dp
    fbuf[own] = total

    def send_piece(i, carry):
        remote(fbuf.at[own], fbuf.at[own], f_send, f_recv, dp_peer(i)).start()
        return carry

    lax.fori_loop(1, OTHERS + 1, send_piece, 0)

    for k in far_first:
        along_z[k].wait_send()
        wait_bytes(wbuf.at[0, 0:OTHERS], b_send.at[k])
    for c in along_y:
        c.wait_send()
    swap.wait_send()
    for group in range(SIDE):
        wait_bytes(gsend.at[0, 0:OTHERS], r_send.at[group])
    wait_bytes(zrecv.at[0:OTHERS], z_send)

    wait_bytes(fbuf.at[0:OTHERS], f_recv)
    for band in range(BANDS):
        at = slice(16 * band, 16 * band + 16)
        grad_in_ref[at, 0:128] = fbuf[band * SLABS]
        grad_in_ref[at, 128:256] = fbuf[band * SLABS + 1]
        grad_in_ref[at, 256:320] = fbuf[band * SLABS + 2][:, 0:64]
        grad_down_ref[at, :] = dot(fbuf[band * SLABS + 2], rgb[...], ((1,), (0,)), precision=HIGH)
    wait_bytes(fbuf.at[0:OTHERS], f_send)


def on_device(loss_scale, features, level_gain, levels, w_in, w_down, w_rgb, target, counts):
    channels, pixels = features.shape[1:]
    rows = w_in.shape[1]
    all_rows = SIDE * SIDE * rows
    group_rows = SIDE * rows
    plane = SIDE * SIDE
    dma = pltpu.SemaphoreType.DMA
    vmem = pl.BlockSpec(memory_space=pltpu.VMEM)
    flops = 2 * all_rows * pixels * (2 * 384 + 3 * 128)
    pred, grad_in, grad_down = pl.pallas_call(
        lambda *refs: kernel(loss_scale, *refs),
        out_shape=(
            jax.ShapeDtypeStruct((3, pixels), F32),
            jax.ShapeDtypeStruct((rows, channels), F32),
            jax.ShapeDtypeStruct((rows, channels), F32),
        ),
        in_specs=[vmem] * 8,
        out_specs=(vmem, vmem, vmem),
        scratch_shapes=[
            pltpu.VMEM((128, channels), F32),
            pltpu.VMEM((384, pixels), BF16),
            pltpu.VMEM((SIDE, plane, SIDE, *TILE), BF16),
            pltpu.VMEM((SIDE, group_rows, 384), BF16),
            pltpu.VMEM((SIDE, group_rows, pixels), BF16),
            pltpu.VMEM((SIDE, group_rows, pixels), F32),
            pltpu.VMEM((8, pixels), F32),
            pltpu.VMEM((8, pixels), F32),
            pltpu.VMEM((16, pixels), F32),
            pltpu.VMEM((128, pixels), BF16),
            pltpu.VMEM((SIDE, plane, SIDE, *TILE), BF16),
            pltpu.VMEM((SIDE, plane, SIDE, *TILE), BF16),
            pltpu.VMEM((SIDE, SIDE, *TILE), F32),
            pltpu.VMEM((plane, *TILE), F32),
            pltpu.VMEM((plane, *TILE), F32),
            dma((SIDE,)), dma((SIDE,)), dma((SIDE,)), dma((SIDE,)), dma((SIDE,)), dma((SIDE,)), dma, dma,
            dma((SIDE,)), dma((SIDE,)), dma, dma, dma, dma,
        ],
        compiler_params=pltpu.CompilerParams(
            collective_id=0, has_side_effects=True, vmem_limit_bytes=56 * 2**20
        ),
        cost_estimate=pl.CostEstimate(flops=flops, bytes_accessed=2**21, transcendentals=all_rows * pixels),
    )(features[0], level_gain, levels[None], w_in[0], w_down[0], w_rgb[0], target, counts[None])
    return pred[None], grad_in[None], grad_down[None]


def solution(mesh):
    in_specs = (
        P("pair", None, ("dp", "fsdp")),
        P(),
        P(),
        P("pair", "fsdp", None),
        P("pair", "fsdp", None),
        P("pair", None, None),
        P(None, ("dp", "fsdp")),
        P(("dp", "fsdp")),
    )
    out_specs = (P("pair", None, ("dp", "fsdp")), P("pair", "fsdp", None), P("pair", "fsdp", None))

    def whole(features, *rest):
        loss_scale = math.sqrt(features.shape[1] / features.shape[2])
        return jax.shard_map(
            lambda *args: on_device(loss_scale, *args),
            mesh=mesh, in_specs=in_specs, out_specs=out_specs, check_vma=False,
        )(features, *rest)

    return whole
```

```python
import math

import jax
import jax.numpy as jnp
from jax import lax
from jax.experimental import pallas as pl
from jax.experimental.pallas import tpu as pltpu
from jax.sharding import PartitionSpec as P

IMG_PIX = 4096
EPS = 1e-06
DISTILL = 1.0

MESH = pl.DeviceIdType.MESH
HIGH = lax.Precision.HIGHEST
BF16 = jnp.bfloat16
F32 = jnp.float32

SIDE = 4
OTHERS = SIDE * SIDE - 1
TILE = (16, 128)
BANDS = 5
SLABS = 3
HEAD = 64


def dot(left, right, dims, **kw):
    return lax.dot_general(left, right, (dims, ((), ())), preferred_element_type=F32, **kw)


def kernel(
    loss_scale,
    x_ref, table_ref, levels_ref, w_in_ref, w_down_ref, w_rgb_ref, target_ref, counts_ref,
    pred_ref, sums_ref,
    rgb, normed, wbuf, wmat, head_t, hidden, slope, pred_mine, pred_other, g_rows, g_aug,
    gsend, grecv, zsend, zrecv, fbuf,
    a_send, a_recv, e_send, e_recv, y_send, y_recv, b_send, b_recv, p_send, p_recv,
    r_send, r_recv, z_send, z_recv, f_send, f_recv,
):
    pair = lax.axis_index("pair")
    dp = lax.axis_index("dp")
    fsdp = lax.axis_index("fsdp")
    x, zl = dp // SIDE, dp % SIDE
    y, zh = fsdp // SIDE, fsdp % SIDE
    here = y * SIDE + x
    pixels = x_ref.shape[1]
    channels = x_ref.shape[0]
    rows = w_in_ref.shape[0]

    def device(x_, y_, zh_, zl_):
        return (pair, x_ * SIDE + zl_, y_ * SIDE + zh_)

    def plane_peer(i):
        return device((x + i % SIDE) % SIDE, (y + i // SIDE) % SIDE, zh, zl)

    def z_peer(i):
        return device(x, y, (zh + i // SIDE) % SIDE, (zl + i % SIDE) % SIDE)

    def dp_peer(i):
        return device((x + i // SIDE) % SIDE, y, zh, (zl + i % SIDE) % SIDE)

    def group_peer(k):
        return device(x, y, (zh + k) % SIDE, zl)

    barrier = pltpu.get_barrier_semaphore()

    def greet(peer):
        pl.semaphore_signal(barrier, inc=1, device_id=peer, device_id_type=MESH)

    def greet_all(i, carry):
        greet(plane_peer(i))
        return carry

    lax.fori_loop(1, OTHERS + 1, greet_all, 0)
    for a in range(SIDE):
        for b in range(1, SIDE):
            greet(dp_peer(a * SIDE + b))
    for k in (1, 3):
        greet(group_peer(k))
    greet((1 - pair, dp, fsdp))

    rgb[...] = jnp.zeros_like(rgb)
    for copy in range(3):
        for k in range(3):
            at = HEAD + 3 * copy + k
            rgb[at : at + 1, :] = w_rgb_ref[k]
    lane = lax.broadcasted_iota(jnp.int32, (rows, 128), 1)
    head = dot(w_down_ref[...].astype(F32), rgb[...], ((1,), (1,)), precision=HIGH)
    head_hi = head.astype(BF16).astype(F32)
    is_lo = (lane >= HEAD + 3) & (lane < HEAD + 6)
    head = jnp.where(is_lo, head - head_hi, head_hi)
    w_own = w_in_ref[...]
    last = w_own[:, 256:320].astype(F32)
    last = jnp.concatenate([last, jnp.zeros((rows, 64), F32)], axis=1) + head
    slabs = [w_own[:, 0:128], w_own[:, 128:256], last.astype(BF16)]
    own_quarters = wbuf.at[zh]
    for band in range(BANDS):
        for slab in range(SLABS):
            q = band * SLABS + slab
            own_quarters[y * SIDE + q // SIDE, q % SIDE] = slabs[slab][16 * band : 16 * band + 16, :]
    own_quarters[y * SIDE + SIDE - 1, SIDE - 1] = jnp.zeros(TILE, BF16)

    pl.semaphore_wait(barrier, OTHERS + 12 + 2 + 1)

    def remote(src, dst, send, recv, peer):
        return pltpu.make_async_remote_copy(
            src_ref=src, dst_ref=dst, send_sem=send, recv_sem=recv,
            device_id=peer, device_id_type=MESH,
        )

    def wait_bytes(ref, sem):
        pltpu.make_async_copy(ref, ref, sem).wait()

    quarter = wbuf.at[zh, here]
    along_z = {}
    for k in (1, 3):
        along_z[k] = remote(quarter, quarter, a_send.at[k], a_recv.at[k], group_peer(k))
        along_z[k].start()
    block = wbuf.at[zh, pl.ds(y * SIDE, SIDE)]
    along_y = []
    for m in range(1, SIDE):
        c = remote(block, block, y_send.at[m], y_recv.at[m], device(x, (y + m) % SIDE, zh, zl))
        c.start()
        along_y.append(c)

    image = ((dp * SIDE * SIDE + fsdp) * pixels) // IMG_PIX
    levels = levels_ref[...].astype(F32)
    spots = lax.broadcasted_iota(jnp.int32, levels.shape, 1)
    level = jnp.sum(jnp.where(spots == image, levels, 0.0), axis=1, keepdims=True)
    table_rows = lax.broadcasted_iota(jnp.int32, table_ref.shape, 0).astype(F32)
    gain = jnp.sum(jnp.where(table_rows == level, table_ref[...], 0.0), axis=0, keepdims=True)
    gain = jnp.concatenate([gain, jnp.zeros((1, 384 - channels), F32)], axis=1)
    gain = jnp.broadcast_to(gain, (128, 384)).T[:channels, 0:1]
    xf = x_ref[...].astype(F32)
    mean_sq = jnp.mean(xf * xf, axis=0, keepdims=True)
    normed[0:channels, :] = (xf * lax.rsqrt(mean_sq + EPS) * gain).astype(BF16)
    normed[channels:, :] = jnp.zeros((384 - channels, pixels), BF16)

    part = rgb[HEAD : HEAD + 16, :]
    part_hi = part.astype(BF16).astype(F32)
    part_mid = (part - part_hi).astype(BF16).astype(F32)
    part_lo = part - part_hi - part_mid
    row = lax.broadcasted_iota(jnp.int32, part.shape, 0)
    part = jnp.where(row < 3, part_hi, jnp.where(row < 6, part_mid, part_lo)).astype(BF16)
    direct = dot(part, x_ref[...], ((1,), (0,)))
    pred_mine[...] = jnp.zeros_like(pred_mine)
    pred_mine[0:3, :] = direct[0:3] + direct[3:6] + direct[6:9]

    wide = 256

    def forward(group):
        def assemble(yy, carry):
            for band in range(BANDS):
                for slab in range(SLABS):
                    q = band * SLABS + slab
                    wmat[group, pl.ds(yy * rows + 16 * band, 16), 128 * slab : 128 * slab + 128] = (
                        wbuf[group, yy * SIDE + q // SIDE, q % SIDE]
                    )
            return carry

        lax.fori_loop(0, SIDE, assemble, 0)
        head_t[group] = wmat[group, :, 256:384].astype(F32).T[HEAD : HEAD + 16].astype(BF16)

        def columns(n, carry):
            at = pl.ds(pl.multiple_of(n * wide, wide), wide)
            pre = dot(wmat[group], normed[:, at], ((1,), (0,)))
            sig = 0.5 * jnp.tanh(0.5 * pre) + 0.5
            act = pre * sig
            hid = act.astype(BF16)
            hidden[group, :, at] = hid
            slope[group, :, at] = sig + act * (1.0 - sig)
            through = dot(head_t[group], hid, ((1,), (0,)))
            pred_mine[0:3, at] += through[0:3] + through[3:6]
            return carry

        lax.fori_loop(0, pixels // wide, columns, 0, unroll=True)

    def forward_on(k):
        group = (zh + SIDE - k) % SIDE
        if k == 2:
            relays[1].wait_recv()
            relays[3].wait_recv()
        else:
            along_z[k].wait_recv()
            half = wbuf.at[group, here, pl.ds(0 if k == 1 else 2, 2)]
            relays[k] = remote(half, half, e_send.at[k], e_recv.at[k], group_peer(k))
            relays[k].start()
        chunk = wbuf.at[group, here]

        def send(i, carry):
            remote(chunk, chunk, b_send.at[k], b_recv.at[k], plane_peer(i)).start()
            return carry

        lax.fori_loop(1, OTHERS + 1, send, 0)

    relays = {}
    for k in (1, 3):
        forward_on(k)
    for c in along_y:
        c.wait_recv()
    forward(zh)
    forward_on(2)
    for k in (1, 3, 2):
        wait_bytes(wbuf.at[0, 0:OTHERS], b_recv.at[k])
        forward((zh + SIDE - k) % SIDE)

    swap = remote(pred_mine, pred_other, p_send, p_recv, (1 - pair, dp, fsdp))
    swap.start()
    pred = pred_mine[0:3, :]
    for k in range(3):
        pred_ref[k] = pred[k : k + 1]
    samples = counts_ref[...].astype(F32)
    weight = samples / (samples + 64.0)
    toward = weight * (pred - target_ref[...])
    swap.wait_recv()
    g_pred = (toward + DISTILL * (pred - pred_other[0:3, :])) * loss_scale
    g_hi = g_pred.astype(BF16).astype(F32)
    g_rows[...] = jnp.zeros_like(g_rows)
    g_rows[0:3, :] = g_hi
    g_rows[3:6, :] = g_hi
    g_rows[6:9, :] = g_pred - g_hi
    g_aug[...] = jnp.zeros_like(g_aug)
    g_aug[HEAD : HEAD + 16, :] = g_rows[...].astype(BF16)

    lane_g = lax.broadcasted_iota(jnp.int32, (SIDE * rows, 128), 1)
    is_rest = (lane_g >= HEAD + 3) & (lane_g < HEAD + 6)

    def backward(group):
        g_hidden = dot(wmat[group, :, 256:384], g_aug[...], ((1,), (0,)))
        g_pre = (g_hidden * slope[group]).astype(BF16)
        grad = dot(g_pre, normed[...], ((1,), (1,)))
        for_head = dot(hidden[group], g_aug[...], ((1,), (1,)))
        for_head = jnp.where(is_rest, for_head - for_head.astype(BF16).astype(F32), for_head)
        out = [
            grad[:, 0:128].astype(BF16),
            grad[:, 128:256].astype(BF16),
            (grad[:, 256:384] + for_head).astype(BF16),
        ]
        for yy in range(SIDE):
            for band in range(BANDS):
                for slab in range(SLABS):
                    q = band * SLABS + slab
                    top = yy * rows + 16 * band
                    gsend[group, yy * SIDE + q // SIDE, q % SIDE] = out[slab][top : top + 16, :]
            gsend[group, yy * SIDE + SIDE - 1, SIDE - 1] = jnp.zeros(TILE, BF16)

        def send(i, carry):
            there = ((y + i // SIDE) % SIDE) * SIDE + (x + i % SIDE) % SIDE
            remote(
                gsend.at[group, there], grecv.at[group, here],
                r_send.at[group], r_recv.at[group], plane_peer(i),
            ).start()
            return carry

        lax.fori_loop(1, OTHERS + 1, send, 0)
        grecv[group, here] = gsend[group, here]

    order = [(zh + k) % SIDE for k in (2, 1, 3, 0)]

    def plane_sum(k, group):
        wait_bytes(grecv.at[0, 0:OTHERS], r_recv.at[group])
        total = grecv[group, 0].astype(F32)
        for s in range(1, SIDE * SIDE):
            total = total + grecv[group, s].astype(F32)
        zsend[group] = total

        def send(b, carry):
            to = (zl + b) % SIDE
            remote(
                zsend.at[group, to], zrecv.at[zh * SIDE + zl], z_send, z_recv, device(x, y, group, to)
            ).start()
            return carry

        lax.fori_loop(1 if k == 0 else 0, SIDE, send, 0)

    for group in order:
        backward(group)
    for k, group in zip((2, 1, 3, 0), order):
        plane_sum(k, group)
    zrecv[zh * SIDE + zl] = zsend[zh, zl]
    wait_bytes(zrecv.at[0:OTHERS], z_recv)
    total = zrecv[0]
    for s in range(1, SIDE * SIDE):
        total = total + zrecv[s]
    own = dp
    fbuf[own] = total

    def send_piece(i, carry):
        remote(fbuf.at[own], fbuf.at[own], f_send, f_recv, dp_peer(i)).start()
        return carry

    lax.fori_loop(1, OTHERS + 1, send_piece, 0)

    for k in (1, 2, 3):
        if k != 2:
            along_z[k].wait_send()
            relays[k].wait_send()
        wait_bytes(wbuf.at[0, 0:OTHERS], b_send.at[k])
    for c in along_y:
        c.wait_send()
    swap.wait_send()
    for group in range(SIDE):
        wait_bytes(gsend.at[0, 0:OTHERS], r_send.at[group])
    wait_bytes(zrecv.at[0:OTHERS], z_send)

    wait_bytes(fbuf.at[0:OTHERS], f_recv)
    sums_ref[...] = fbuf[...]
    wait_bytes(fbuf.at[0:OTHERS], f_send)


def results(sums_ref, pred_in_ref, w_rgb_ref, pred_ref, grad_in_ref, grad_down_ref, rgb):
    pred_ref[...] = pred_in_ref[...]
    rgb[...] = jnp.zeros_like(rgb)
    for copy in range(3):
        for k in range(3):
            at = HEAD + 3 * copy + k
            rgb[at : at + 1, :] = w_rgb_ref[k]
    for band in range(BANDS):
        at = slice(16 * band, 16 * band + 16)
        grad_in_ref[at, 0:128] = sums_ref[band * SLABS]
        grad_in_ref[at, 128:256] = sums_ref[band * SLABS + 1]
        grad_in_ref[at, 256:320] = sums_ref[band * SLABS + 2][:, 0:64]
    last = jnp.concatenate([sums_ref[band * SLABS + 2] for band in range(BANDS)], axis=0)
    grad_down_ref[...] = dot(last, rgb[...], ((1,), (0,)), precision=HIGH)


def on_device(loss_scale, features, level_gain, levels, w_in, w_down, w_rgb, target, counts):
    channels, pixels = features.shape[1:]
    rows = w_in.shape[1]
    all_rows = SIDE * SIDE * rows
    group_rows = SIDE * rows
    plane = SIDE * SIDE
    dma = pltpu.SemaphoreType.DMA
    vmem = pl.BlockSpec(memory_space=pltpu.VMEM)
    flops = 2 * all_rows * pixels * (2 * 384 + 3 * 128)
    colours = jnp.transpose(w_rgb, (1, 0, 2))
    pred, sums = pl.pallas_call(
        lambda *refs: kernel(loss_scale, *refs),
        out_shape=(
            jax.ShapeDtypeStruct((3, 1, pixels), F32),
            jax.ShapeDtypeStruct((plane, *TILE), F32),
        ),
        in_specs=[vmem] * 8,
        out_specs=(vmem, vmem),
        scratch_shapes=[
            pltpu.VMEM((128, channels), F32),
            pltpu.VMEM((384, pixels), BF16),
            pltpu.VMEM((SIDE, plane, SIDE, *TILE), BF16),
            pltpu.VMEM((SIDE, group_rows, 384), BF16),
            pltpu.VMEM((SIDE, 16, group_rows), BF16),
            pltpu.VMEM((SIDE, group_rows, pixels), BF16),
            pltpu.VMEM((SIDE, group_rows, pixels), F32),
            pltpu.VMEM((8, pixels), F32),
            pltpu.VMEM((8, pixels), F32),
            pltpu.VMEM((16, pixels), F32),
            pltpu.VMEM((128, pixels), BF16),
            pltpu.VMEM((SIDE, plane, SIDE, *TILE), BF16),
            pltpu.VMEM((SIDE, plane, SIDE, *TILE), BF16),
            pltpu.VMEM((SIDE, SIDE, *TILE), F32),
            pltpu.VMEM((plane, *TILE), F32),
            pltpu.VMEM((plane, *TILE), F32),
            dma((SIDE,)), dma((SIDE,)), dma((SIDE,)), dma((SIDE,)),
            dma((SIDE,)), dma((SIDE,)), dma((SIDE,)), dma((SIDE,)), dma, dma,
            dma((SIDE,)), dma((SIDE,)), dma, dma, dma, dma,
        ],
        compiler_params=pltpu.CompilerParams(
            collective_id=0, has_side_effects=True, vmem_limit_bytes=56 * 2**20
        ),
        cost_estimate=pl.CostEstimate(flops=flops, bytes_accessed=2**21, transcendentals=all_rows * pixels),
    )(features[0], level_gain, levels[None], w_in[0], w_down[0], colours, target, counts[None])
    pred, grad_in, grad_down = pl.pallas_call(
        results,
        out_shape=(
            jax.ShapeDtypeStruct((3, 1, pixels), F32),
            jax.ShapeDtypeStruct((rows, channels), F32),
            jax.ShapeDtypeStruct((rows, channels), F32),
        ),
        in_specs=[vmem] * 3,
        out_specs=(vmem, vmem, vmem),
        scratch_shapes=[pltpu.VMEM((128, channels), F32)],
    )(sums, pred, colours)
    return jnp.transpose(pred, (1, 0, 2)), grad_in[None], grad_down[None]


def solution(mesh):
    in_specs = (
        P("pair", None, ("dp", "fsdp")),
        P(),
        P(),
        P("pair", "fsdp", None),
        P("pair", "fsdp", None),
        P("pair", None, None),
        P(None, ("dp", "fsdp")),
        P(("dp", "fsdp")),
    )
    out_specs = (P("pair", None, ("dp", "fsdp")), P("pair", "fsdp", None), P("pair", "fsdp", None))

    def whole(features, *rest):
        loss_scale = math.sqrt(features.shape[1] / features.shape[2])
        return jax.shard_map(
            lambda *args: on_device(loss_scale, *args),
            mesh=mesh, in_specs=in_specs, out_specs=out_specs, check_vma=False,
        )(features, *rest)

    return whole
```

```python
import math

import jax
import jax.numpy as jnp
from jax import lax
from jax.experimental import pallas as pl
from jax.experimental.pallas import tpu as pltpu
from jax.sharding import PartitionSpec as P

IMG_PIX = 4096
EPS = 1e-06
DISTILL = 1.0

MESH = pl.DeviceIdType.MESH
HIGH = lax.Precision.HIGHEST
BF16 = jnp.bfloat16
F32 = jnp.float32

SIDE = 4
OTHERS = SIDE * SIDE - 1
TILE = (16, 128)
BANDS = 5
HEAD = 64
PARTS = 9
SHARE = 3
TILES = SIDE * SHARE + 1


def pack(slab0, slab1, last, head):
    band = [slice(16 * b, 16 * b + 16) for b in range(BANDS)]
    tiles = [slab0[at] for at in band] + [slab1[at] for at in band]
    tiles.append(last[band[0]] + pltpu.roll(last[band[1]], 64, 1))
    tiles.append(last[band[2]] + pltpu.roll(last[band[3]], 64, 1))
    end = last[band[4]] + head[band[0]]
    for b in range(1, BANDS):
        end = end + pltpu.roll(head[band[b]], PARTS * b, 1)
    return [t.astype(BF16) for t in tiles] + [end.astype(BF16)]


def unpack_last(ten, eleven, end):
    lane = lax.broadcasted_iota(jnp.int32, TILE, 1)
    values = [ten, pltpu.roll(ten, 64, 1), eleven, pltpu.roll(eleven, 64, 1), end]
    heads = [end] + [pltpu.roll(end, 128 - PARTS * b, 1) for b in range(1, BANDS)]
    return [jnp.where(lane < HEAD, v, h) for v, h in zip(values, heads)]


def dot(left, right, dims, **kw):
    return lax.dot_general(left, right, (dims, ((), ())), preferred_element_type=F32, **kw)


def kernel(
    loss_scale,
    x_ref, table_ref, levels_ref, w_in_ref, w_down_ref, w_rgb_ref, target_ref, counts_ref,
    pred_ref, sums_ref,
    rgb, normed, wbuf, wext, wmat, head_t, hidden, slope, pred_mine, pred_other, g_rows, g_aug,
    gsend, gext, grecv, xrecv, zsend, zext, zrecv, fbuf,
    ax_send, ax_recv, ex_send, ex_recv, yx_send, yx_recv, bx_send, bx_recv, rx_send, rx_recv,
    a_send, a_recv, e_send, e_recv, y_send, y_recv, b_send, b_recv, p_send, p_recv,
    r_send, r_recv, z_send, z_recv, f_send, f_recv,
):
    pair = lax.axis_index("pair")
    dp = lax.axis_index("dp")
    fsdp = lax.axis_index("fsdp")
    x, zl = dp // SIDE, dp % SIDE
    y, zh = fsdp // SIDE, fsdp % SIDE
    here = y * SIDE + x
    pixels = x_ref.shape[1]
    channels = x_ref.shape[0]
    rows = w_in_ref.shape[0]

    def device(x_, y_, zh_, zl_):
        return (pair, x_ * SIDE + zl_, y_ * SIDE + zh_)

    def plane_peer(i):
        return device((x + i % SIDE) % SIDE, (y + i // SIDE) % SIDE, zh, zl)

    def z_peer(i):
        return device(x, y, (zh + i // SIDE) % SIDE, (zl + i % SIDE) % SIDE)

    def dp_peer(i):
        return device((x + i // SIDE) % SIDE, y, zh, (zl + i % SIDE) % SIDE)

    def group_peer(k):
        return device(x, y, (zh + k) % SIDE, zl)

    barrier = pltpu.get_barrier_semaphore()

    def greet(peer):
        pl.semaphore_signal(barrier, inc=1, device_id=peer, device_id_type=MESH)

    def greet_all(i, carry):
        greet(plane_peer(i))
        return carry

    lax.fori_loop(1, OTHERS + 1, greet_all, 0)
    for a in range(SIDE):
        for b in range(1, SIDE):
            greet(dp_peer(a * SIDE + b))
    for k in (1, 3):
        greet(group_peer(k))
    greet((1 - pair, dp, fsdp))

    rgb[...] = jnp.zeros_like(rgb)
    for copy in range(3):
        for k in range(3):
            at = HEAD + 3 * copy + k
            rgb[at : at + 1, :] = w_rgb_ref[k]
    lane = lax.broadcasted_iota(jnp.int32, (rows, 128), 1)
    head = dot(w_down_ref[...].astype(F32), rgb[...], ((1,), (1,)), precision=HIGH)
    head_hi = head.astype(BF16).astype(F32)
    is_lo = (lane >= HEAD + 3) & (lane < HEAD + 6)
    head = jnp.where(is_lo, head - head_hi, head_hi)
    w_own = w_in_ref[...]
    last = w_own[:, 256:320].astype(F32)
    last = jnp.concatenate([last, jnp.zeros((rows, 64), F32)], axis=1)
    tiles = pack(w_own[:, 0:128], w_own[:, 128:256], last, head)
    for t in range(TILES - 1):
        wbuf[zh, y * SIDE + t // SHARE, t % SHARE] = tiles[t]
    wext[zh, y] = tiles[-1]

    pl.semaphore_wait(barrier, OTHERS + 12 + 2 + 1)

    def remote(src, dst, send, recv, peer):
        return pltpu.make_async_remote_copy(
            src_ref=src, dst_ref=dst, send_sem=send, recv_sem=recv,
            device_id=peer, device_id_type=MESH,
        )

    def wait_bytes(ref, sem):
        pltpu.make_async_copy(ref, ref, sem).wait()

    quarter = wbuf.at[zh, here]
    along_z = {}
    for k in (1, 3):
        along_z[k] = remote(quarter, quarter, a_send.at[k], a_recv.at[k], group_peer(k))
        along_z[k].start()

    def when_mine(group, copy):
        @pl.when(x == group)
        def _():
            copy()

    along_z_ext = {}
    for k in (1, 3):
        along_z_ext[k] = remote(wext.at[zh, y], wext.at[zh, y], ax_send.at[k], ax_recv.at[k], group_peer(k))
        when_mine(zh, along_z_ext[k].start)
    block = wbuf.at[zh, pl.ds(y * SIDE, SIDE)]
    along_y = []
    for m in range(1, SIDE):
        c = remote(block, block, y_send.at[m], y_recv.at[m], device(x, (y + m) % SIDE, zh, zl))
        c.start()
        along_y.append(c)
        peer = device(x, (y + m) % SIDE, zh, zl)
        c = remote(wext.at[zh, y], wext.at[zh, y], yx_send.at[m], yx_recv.at[m], peer)
        c.start()
        along_y.append(c)

    image = ((dp * SIDE * SIDE + fsdp) * pixels) // IMG_PIX
    levels = levels_ref[...].astype(F32)
    spots = lax.broadcasted_iota(jnp.int32, levels.shape, 1)
    level = jnp.sum(jnp.where(spots == image, levels, 0.0), axis=1, keepdims=True)
    table_rows = lax.broadcasted_iota(jnp.int32, table_ref.shape, 0).astype(F32)
    gain = jnp.sum(jnp.where(table_rows == level, table_ref[...], 0.0), axis=0, keepdims=True)
    gain = jnp.concatenate([gain, jnp.zeros((1, 384 - channels), F32)], axis=1)
    gain = jnp.broadcast_to(gain, (128, 384)).T[:channels, 0:1]
    xf = x_ref[...].astype(F32)
    mean_sq = jnp.mean(xf * xf, axis=0, keepdims=True)
    normed[0:channels, :] = (xf * lax.rsqrt(mean_sq + EPS) * gain).astype(BF16)
    normed[channels:, :] = jnp.zeros((384 - channels, pixels), BF16)

    part = rgb[HEAD : HEAD + 16, :]
    part_hi = part.astype(BF16).astype(F32)
    part_mid = (part - part_hi).astype(BF16).astype(F32)
    part_lo = part - part_hi - part_mid
    row = lax.broadcasted_iota(jnp.int32, part.shape, 0)
    part = jnp.where(row < 3, part_hi, jnp.where(row < 6, part_mid, part_lo)).astype(BF16)
    direct = dot(part, x_ref[...], ((1,), (0,)))
    pred_mine[...] = jnp.zeros_like(pred_mine)
    pred_mine[0:3, :] = direct[0:3] + direct[3:6] + direct[6:9]

    wide = 256

    def forward(group):
        def assemble(yy, carry):
            def tile(t):
                return wbuf[group, yy * SIDE + t // SHARE, t % SHARE]

            end = unpack_last(tile(10).astype(F32), tile(11).astype(F32), wext[group, yy].astype(F32))
            for band in range(BANDS):
                at = pl.ds(yy * rows + 16 * band, 16)
                wmat[group, at, 0:128] = tile(band)
                wmat[group, at, 128:256] = tile(BANDS + band)
                wmat[group, at, 256:384] = end[band].astype(BF16)
            return carry

        lax.fori_loop(0, SIDE, assemble, 0)
        head_t[group] = wmat[group, :, 256:384].astype(F32).T[HEAD : HEAD + 16].astype(BF16)

        def columns(n, carry):
            at = pl.ds(pl.multiple_of(n * wide, wide), wide)
            pre = dot(wmat[group], normed[:, at], ((1,), (0,)))
            sig = 0.5 * jnp.tanh(0.5 * pre) + 0.5
            act = pre * sig
            hid = act.astype(BF16)
            hidden[group, :, at] = hid
            slope[group, :, at] = sig + act * (1.0 - sig)
            through = dot(head_t[group], hid, ((1,), (0,)))
            pred_mine[0:3, at] += through[0:3] + through[3:6]
            return carry

        lax.fori_loop(0, pixels // wide, columns, 0, unroll=True)

    def forward_on(k):
        group = (zh + SIDE - k) % SIDE
        if k == 2:
            relays[1].wait_recv()
            relays[3].wait_recv()
            when_mine(group, relay_ext.wait_recv)
        else:
            along_z[k].wait_recv()
            when_mine(group, along_z_ext[k].wait_recv)
            some = wbuf.at[group, here, pl.ds(0, 2) if k == 1 else pl.ds(2, 1)]
            relays[k] = remote(some, some, e_send.at[k], e_recv.at[k], group_peer(k))
            relays[k].start()
            if k == 3:
                when_mine(group, relay_ext.start)
        chunk = wbuf.at[group, here]
        extra = wext.at[group, y]

        def send(i, carry):
            remote(chunk, chunk, b_send.at[k], b_recv.at[k], plane_peer(i)).start()
            when_mine(group, remote(extra, extra, bx_send.at[k], bx_recv.at[k], plane_peer(i)).start)
            return carry

        lax.fori_loop(1, OTHERS + 1, send, 0)

    def wait_group(k):
        group = (zh + SIDE - k) % SIDE
        wait_bytes(wbuf.at[0, 0:OTHERS], b_recv.at[k])

        @pl.when(x == group)
        def _():
            wait_bytes(wext.at[0, 0 : SIDE - 1], bx_recv.at[k])

        @pl.when(x != group)
        def _():
            wait_bytes(wext.at[0], bx_recv.at[k])

    relays = {}
    passed = wext.at[(zh + 1) % SIDE, y]
    relay_ext = remote(passed, passed, ex_send, ex_recv, group_peer(3))
    for k in (1, 3):
        forward_on(k)
    for c in along_y:
        c.wait_recv()
    forward(zh)
    forward_on(2)
    for k in (1, 3, 2):
        wait_group(k)
        forward((zh + SIDE - k) % SIDE)

    swap = remote(pred_mine, pred_other, p_send, p_recv, (1 - pair, dp, fsdp))
    swap.start()
    pred = pred_mine[0:3, :]
    for k in range(3):
        pred_ref[k] = pred[k : k + 1]
    samples = counts_ref[...].astype(F32)
    weight = samples / (samples + 64.0)
    toward = weight * (pred - target_ref[...])
    swap.wait_recv()
    g_pred = (toward + DISTILL * (pred - pred_other[0:3, :])) * loss_scale
    g_hi = g_pred.astype(BF16).astype(F32)
    g_rows[...] = jnp.zeros_like(g_rows)
    g_rows[0:3, :] = g_hi
    g_rows[3:6, :] = g_hi
    g_rows[6:9, :] = g_pred - g_hi
    g_aug[...] = jnp.zeros_like(g_aug)
    g_aug[HEAD : HEAD + 16, :] = g_rows[...].astype(BF16)

    lane_g = lax.broadcasted_iota(jnp.int32, (SIDE * rows, 128), 1)
    is_rest = (lane_g >= HEAD + 3) & (lane_g < HEAD + 6)

    def backward(group):
        g_hidden = dot(wmat[group, :, 256:384], g_aug[...], ((1,), (0,)))
        g_pre = (g_hidden * slope[group]).astype(BF16)
        grad = dot(g_pre, normed[...], ((1,), (1,)))
        for_head = dot(hidden[group], g_aug[...], ((1,), (1,)))
        for_head = jnp.where(is_rest, for_head - for_head.astype(BF16).astype(F32), for_head)
        for yy in range(SIDE):
            at = slice(yy * rows, yy * rows + rows)
            tiles = pack(grad[at, 0:128], grad[at, 128:256], grad[at, 256:384], for_head[at])
            for t in range(TILES - 1):
                gsend[group, yy * SIDE + t // SHARE, t % SHARE] = tiles[t]
            gext[group, yy] = tiles[-1]

        def send(i, carry):
            there = ((y + i // SIDE) % SIDE) * SIDE + (x + i % SIDE) % SIDE
            remote(
                gsend.at[group, there], grecv.at[group, here],
                r_send.at[group], r_recv.at[group], plane_peer(i),
            ).start()
            return carry

        lax.fori_loop(1, OTHERS + 1, send, 0)
        grecv[group, here] = gsend[group, here]

        def send_ext(b, carry):
            to = (y + b) % SIDE
            remote(
                gext.at[group, to], xrecv.at[here], rx_send.at[group], rx_recv, device(group, to, zh, zl)
            ).start()
            return carry

        @pl.when(x == group)
        def _():
            lax.fori_loop(1, SIDE, send_ext, 0)
            xrecv[here] = gext[group, y]

        @pl.when(x != group)
        def _():
            lax.fori_loop(0, SIDE, send_ext, 0)

    order = [(zh + k) % SIDE for k in (2, 1, 3, 0)]

    def plane_sum(group):
        wait_bytes(grecv.at[0, 0:OTHERS], r_recv.at[group])
        total = grecv[group, 0].astype(F32)
        for s in range(1, SIDE * SIDE):
            total = total + grecv[group, s].astype(F32)
        zsend[group] = total

        own_slot = zrecv.at[zh * SIDE + zl]

        def send(to, carry):
            @pl.when((group != zh) | (to != zl))
            def _():
                remote(zsend.at[group, to], own_slot, z_send, z_recv, device(x, y, group, to)).start()

            return carry

        lax.fori_loop(0, SHARE, send, 0)

        @pl.when(x == group)
        def _():
            wait_bytes(xrecv.at[0:OTHERS], rx_recv)
            total = xrecv[0].astype(F32)
            for s in range(1, SIDE * SIDE):
                total = total + xrecv[s].astype(F32)
            zext[...] = total

            @pl.when((group != zh) | (zl != SHARE))
            def _():
                remote(zext, own_slot, z_send, z_recv, device(x, y, group, SHARE)).start()

    for group in order:
        backward(group)
    for group in order:
        plane_sum(group)
    has_tile = (zl < SHARE) | (x == zh)

    @pl.when(zl < SHARE)
    def _():
        zrecv[zh * SIDE + zl] = zsend[zh, zl]

    @pl.when((zl == SHARE) & (x == zh))
    def _():
        zrecv[zh * SIDE + zl] = zext[...]

    @pl.when(has_tile)
    def _():
        wait_bytes(zrecv.at[0:OTHERS], z_recv)
        total = zrecv[0]
        for s in range(1, SIDE * SIDE):
            total = total + zrecv[s]
        own = jnp.where(zl < SHARE, x * SHARE + zl, TILES - 1)
        fbuf[own] = total

        def send_piece(i, carry):
            remote(fbuf.at[own], fbuf.at[own], f_send, f_recv, dp_peer(i)).start()
            return carry

        lax.fori_loop(1, OTHERS + 1, send_piece, 0)

    for k in (1, 2, 3):
        group = (zh + SIDE - k) % SIDE
        if k != 2:
            along_z[k].wait_send()
            when_mine(zh, along_z_ext[k].wait_send)
            relays[k].wait_send()
        wait_bytes(wbuf.at[0, 0:OTHERS], b_send.at[k])
        when_mine(group, lambda: wait_bytes(xrecv.at[0:OTHERS], bx_send.at[k]))
    when_mine((zh + 1) % SIDE, relay_ext.wait_send)
    for c in along_y:
        c.wait_send()
    swap.wait_send()
    for group in range(SIDE):
        wait_bytes(gsend.at[0, 0:OTHERS], r_send.at[group])

        @pl.when(x == group)
        def _():
            wait_bytes(gext.at[0, 0 : SIDE - 1], rx_send.at[group])

        @pl.when(x != group)
        def _():
            wait_bytes(gext.at[0], rx_send.at[group])

    @pl.when(has_tile)
    def _():
        wait_bytes(fbuf.at[0 : TILES - 1], z_send)
        wait_bytes(fbuf.at[0 : TILES - 1], f_recv)
        wait_bytes(zrecv.at[0:OTHERS], f_send)

    @pl.when(jnp.logical_not(has_tile))
    def _():
        wait_bytes(fbuf, z_send)
        wait_bytes(fbuf, f_recv)

    sums_ref[...] = fbuf[...]


def results(sums_ref, pred_in_ref, w_rgb_ref, pred_ref, grad_in_ref, grad_down_ref, rgb):
    pred_ref[...] = pred_in_ref[...]
    rgb[...] = jnp.zeros_like(rgb)
    for copy in range(3):
        for k in range(3):
            at = HEAD + 3 * copy + k
            rgb[at : at + 1, :] = w_rgb_ref[k]
    end = unpack_last(sums_ref[10], sums_ref[11], sums_ref[12])
    for band in range(BANDS):
        at = slice(16 * band, 16 * band + 16)
        grad_in_ref[at, 0:128] = sums_ref[band]
        grad_in_ref[at, 128:256] = sums_ref[BANDS + band]
        grad_in_ref[at, 256:320] = end[band][:, 0:64]
    last = jnp.concatenate(end, axis=0)
    grad_down_ref[...] = dot(last, rgb[...], ((1,), (0,)), precision=HIGH)


def on_device(loss_scale, features, level_gain, levels, w_in, w_down, w_rgb, target, counts):
    channels, pixels = features.shape[1:]
    rows = w_in.shape[1]
    all_rows = SIDE * SIDE * rows
    group_rows = SIDE * rows
    plane = SIDE * SIDE
    dma = pltpu.SemaphoreType.DMA
    vmem = pl.BlockSpec(memory_space=pltpu.VMEM)
    flops = 2 * all_rows * pixels * (2 * 384 + 3 * 128)
    colours = jnp.transpose(w_rgb, (1, 0, 2))
    pred, sums = pl.pallas_call(
        lambda *refs: kernel(loss_scale, *refs),
        out_shape=(
            jax.ShapeDtypeStruct((3, 1, pixels), F32),
            jax.ShapeDtypeStruct((TILES, *TILE), F32),
        ),
        in_specs=[vmem] * 8,
        out_specs=(vmem, vmem),
        scratch_shapes=[
            pltpu.VMEM((128, channels), F32),
            pltpu.VMEM((384, pixels), BF16),
            pltpu.VMEM((SIDE, plane, SHARE, *TILE), BF16),
            pltpu.VMEM((SIDE, SIDE, *TILE), BF16),
            pltpu.VMEM((SIDE, group_rows, 384), BF16),
            pltpu.VMEM((SIDE, 16, group_rows), BF16),
            pltpu.VMEM((SIDE, group_rows, pixels), BF16),
            pltpu.VMEM((SIDE, group_rows, pixels), F32),
            pltpu.VMEM((8, pixels), F32),
            pltpu.VMEM((8, pixels), F32),
            pltpu.VMEM((16, pixels), F32),
            pltpu.VMEM((128, pixels), BF16),
            pltpu.VMEM((SIDE, plane, SHARE, *TILE), BF16),
            pltpu.VMEM((SIDE, SIDE, *TILE), BF16),
            pltpu.VMEM((SIDE, plane, SHARE, *TILE), BF16),
            pltpu.VMEM((plane, *TILE), BF16),
            pltpu.VMEM((SIDE, SHARE, *TILE), F32),
            pltpu.VMEM(TILE, F32),
            pltpu.VMEM((plane, *TILE), F32),
            pltpu.VMEM((TILES, *TILE), F32),
            dma((SIDE,)), dma((SIDE,)), dma, dma, dma((SIDE,)), dma((SIDE,)), dma((SIDE,)), dma((SIDE,)), dma((SIDE,)), dma,
            dma((SIDE,)), dma((SIDE,)), dma((SIDE,)), dma((SIDE,)),
            dma((SIDE,)), dma((SIDE,)), dma((SIDE,)), dma((SIDE,)), dma, dma,
            dma((SIDE,)), dma((SIDE,)), dma, dma, dma, dma,
        ],
        compiler_params=pltpu.CompilerParams(
            collective_id=0, has_side_effects=True, vmem_limit_bytes=56 * 2**20
        ),
        cost_estimate=pl.CostEstimate(flops=flops, bytes_accessed=2**21, transcendentals=all_rows * pixels),
    )(features[0], level_gain, levels[None], w_in[0], w_down[0], colours, target, counts[None])
    pred, grad_in, grad_down = pl.pallas_call(
        results,
        out_shape=(
            jax.ShapeDtypeStruct((3, 1, pixels), F32),
            jax.ShapeDtypeStruct((rows, channels), F32),
            jax.ShapeDtypeStruct((rows, channels), F32),
        ),
        in_specs=[vmem] * 3,
        out_specs=(vmem, vmem, vmem),
        scratch_shapes=[pltpu.VMEM((128, channels), F32)],
    )(sums, pred, colours)
    return jnp.transpose(pred, (1, 0, 2)), grad_in[None], grad_down[None]


def solution(mesh):
    in_specs = (
        P("pair", None, ("dp", "fsdp")),
        P(),
        P(),
        P("pair", "fsdp", None),
        P("pair", "fsdp", None),
        P("pair", None, None),
        P(None, ("dp", "fsdp")),
        P(("dp", "fsdp")),
    )
    out_specs = (P("pair", None, ("dp", "fsdp")), P("pair", "fsdp", None), P("pair", "fsdp", None))

    def whole(features, *rest):
        loss_scale = math.sqrt(features.shape[1] / features.shape[2])
        return jax.shard_map(
            lambda *args: on_device(loss_scale, *args),
            mesh=mesh, in_specs=in_specs, out_specs=out_specs, check_vma=False,
        )(features, *rest)

    return whole
```

```python
import math

import jax
import jax.numpy as jnp
from jax import lax
from jax.experimental import pallas as pl
from jax.experimental.pallas import tpu as pltpu
from jax.sharding import PartitionSpec as P

IMG_PIX = 4096
EPS = 1e-06
DISTILL = 1.0

MESH = pl.DeviceIdType.MESH
HIGH = lax.Precision.HIGHEST
BF16 = jnp.bfloat16
F32 = jnp.float32

SIDE = 4
OTHERS = SIDE * SIDE - 1
TILE = (16, 128)
BANDS = 5
HEAD = 64
PARTS = 9
SHARE = 3
TILES = SIDE * SHARE + 1


def pack(slab0, slab1, last):
    band = [slice(16 * b, 16 * b + 16) for b in range(BANDS)]
    tiles = [slab0[at] for at in band] + [slab1[at] for at in band]
    tiles.append(last[band[0]] + pltpu.roll(last[band[1]], 64, 1))
    tiles.append(last[band[2]] + pltpu.roll(last[band[3]], 64, 1))
    return [t.astype(BF16) for t in tiles]


def pack_end(last, head):
    band = [slice(16 * b, 16 * b + 16) for b in range(BANDS)]
    end = last[band[4]] + head[band[0]]
    for b in range(1, BANDS):
        end = end + pltpu.roll(head[band[b]], PARTS * b, 1)
    return end.astype(BF16)


def unpack_last(ten, eleven, end):
    lane = lax.broadcasted_iota(jnp.int32, TILE, 1)
    values = [ten, pltpu.roll(ten, 64, 1), eleven, pltpu.roll(eleven, 64, 1), end]
    heads = [end] + [pltpu.roll(end, 128 - PARTS * b, 1) for b in range(1, BANDS)]
    return [jnp.where(lane < HEAD, v, h) for v, h in zip(values, heads)]


def dot(left, right, dims, **kw):
    return lax.dot_general(left, right, (dims, ((), ())), preferred_element_type=F32, **kw)


def kernel(
    loss_scale,
    x_hbm, table_hbm, w_in_hbm, w_down_hbm, levels_ref, w_rgb_ref, target_ref, counts_ref,
    pred_ref, sums_ref,
    x_ref, table_ref, w_in_ref, w_down_ref, in_sem,
    rgb_rows, rgb_parts, normed, wbuf, wext, wmat, head_t, hidden, slope, pred_mine, pred_other, g_rows, g_aug,
    gsend, gext, grecv, xrecv, zsend, zext, zrecv, fbuf,
    ax_send, ax_recv, ex_send, ex_recv, yx_send, yx_recv, bx_send, bx_recv, rx_send, rx_recv,
    a_send, a_recv, e_send, e_recv, y_send, y_recv, b_send, b_recv, p_send, p_recv,
    r_send, r_recv, z_send, z_recv, f_send, f_recv,
):
    pair = lax.axis_index("pair")
    dp = lax.axis_index("dp")
    fsdp = lax.axis_index("fsdp")
    x, zl = dp // SIDE, dp % SIDE
    y, zh = fsdp // SIDE, fsdp % SIDE
    here = y * SIDE + x
    channels, pixels = x_ref.shape
    rows = w_in_ref.shape[0]

    def device(x_, y_, zh_, zl_):
        return (pair, x_ * SIDE + zl_, y_ * SIDE + zh_)

    def plane_peer(i):
        return device((x + i % SIDE) % SIDE, (y + i // SIDE) % SIDE, zh, zl)

    def z_peer(i):
        return device(x, y, (zh + i // SIDE) % SIDE, (zl + i % SIDE) % SIDE)

    def dp_peer(i):
        return device((x + i // SIDE) % SIDE, y, zh, (zl + i % SIDE) % SIDE)

    def group_peer(k):
        return device(x, y, (zh + k) % SIDE, zl)

    loads = {}
    for n, (src, dst) in enumerate(
        ((w_in_hbm, w_in_ref), (w_down_hbm, w_down_ref), (x_hbm, x_ref), (table_hbm, table_ref))
    ):
        loads[n] = pltpu.make_async_copy(src, dst, in_sem.at[n])
        loads[n].start()

    barrier = pltpu.get_barrier_semaphore()

    def greet(peer):
        pl.semaphore_signal(barrier, inc=1, device_id=peer, device_id_type=MESH)

    def greet_all(i, carry):
        greet(plane_peer(i))
        return carry

    lax.fori_loop(1, OTHERS + 1, greet_all, 0)
    for a in range(SIDE):
        for b in range(1, SIDE):
            greet(dp_peer(a * SIDE + b))
    for k in (1, 3):
        greet(group_peer(k))
    greet((1 - pair, dp, fsdp))

    loads[0].wait()
    w_own = w_in_ref[...]
    last = w_own[:, 256:320].astype(F32)
    last = jnp.concatenate([last, jnp.zeros((rows, 64), F32)], axis=1)
    tiles = pack(w_own[:, 0:128], w_own[:, 128:256], last)
    for t in range(TILES - 1):
        wbuf[zh, y * SIDE + t // SHARE, t % SHARE] = tiles[t]

    pl.semaphore_wait(barrier, OTHERS + 12 + 2 + 1)

    def remote(src, dst, send, recv, peer):
        return pltpu.make_async_remote_copy(
            src_ref=src, dst_ref=dst, send_sem=send, recv_sem=recv,
            device_id=peer, device_id_type=MESH,
        )

    def wait_bytes(ref, sem):
        pltpu.make_async_copy(ref, ref, sem).wait()

    quarter = wbuf.at[zh, here]
    along_z = {}
    for k in (1, 3):
        along_z[k] = remote(quarter, quarter, a_send.at[k], a_recv.at[k], group_peer(k))
        along_z[k].start()

    def when_mine(group, copy):
        @pl.when(x == group)
        def _():
            copy()

    block = wbuf.at[zh, pl.ds(y * SIDE, SIDE)]
    along_y = []
    for m in range(1, SIDE):
        c = remote(block, block, y_send.at[m], y_recv.at[m], device(x, (y + m) % SIDE, zh, zl))
        c.start()
        along_y.append(c)

    rgb_rows[...] = jnp.zeros_like(rgb_rows)
    for copy in range(3):
        for k in range(3):
            at = 3 * copy + k
            rgb_rows[at : at + 1, :] = w_rgb_ref[k]
    part = rgb_rows[...]
    part_hi = part.astype(BF16).astype(F32)
    part_mid = (part - part_hi).astype(BF16).astype(F32)
    part_lo = part - part_hi - part_mid
    rgb_parts[...] = jnp.zeros_like(rgb_parts)
    for n, p in enumerate((part_hi, part_mid, part_lo)):
        rgb_parts[HEAD + 16 * n : HEAD + 16 * n + 16, :] = p.astype(BF16)
    loads[1].wait()
    head = dot(w_down_ref[...], rgb_parts[...], ((1,), (1,)))
    head = head + pltpu.roll(head, 112, 1) + pltpu.roll(head, 96, 1)
    lane = lax.broadcasted_iota(jnp.int32, (rows, 128), 1)
    head = jnp.where((lane >= HEAD) & (lane < HEAD + PARTS), head, 0.0)
    head_hi = head.astype(BF16).astype(F32)
    is_lo = (lane >= HEAD + 3) & (lane < HEAD + 6)
    head = jnp.where(is_lo, head - head_hi, head_hi)
    own_ext = wext.at[zh, y]
    own_ext[...] = pack_end(last, head)
    along_z_ext = {}
    for k in (1, 3):
        along_z_ext[k] = remote(own_ext, own_ext, ax_send.at[k], ax_recv.at[k], group_peer(k))
        when_mine(zh, along_z_ext[k].start)
    for m in range(1, SIDE):
        peer = device(x, (y + m) % SIDE, zh, zl)
        c = remote(own_ext, own_ext, yx_send.at[m], yx_recv.at[m], peer)
        c.start()
        along_y.append(c)

    loads[2].wait()
    loads[3].wait()
    image = ((dp * SIDE * SIDE + fsdp) * pixels) // IMG_PIX
    levels = levels_ref[...].astype(F32)
    spots = lax.broadcasted_iota(jnp.int32, levels.shape, 1)
    level = jnp.sum(jnp.where(spots == image, levels, 0.0), axis=1, keepdims=True)
    table_rows = lax.broadcasted_iota(jnp.int32, table_ref.shape, 0).astype(F32)
    gain = jnp.sum(jnp.where(table_rows == level, table_ref[...], 0.0), axis=0, keepdims=True)
    gain = jnp.concatenate([gain, jnp.zeros((1, 384 - channels), F32)], axis=1)
    gain = jnp.broadcast_to(gain, (128, 384)).T[:channels, 0:1]
    xf = x_ref[...].astype(F32)
    mean_sq = jnp.mean(xf * xf, axis=0, keepdims=True)
    normed[0:channels, :] = (xf * lax.rsqrt(mean_sq + EPS) * gain).astype(BF16)
    normed[channels:, :] = jnp.zeros((384 - channels, pixels), BF16)

    row = lax.broadcasted_iota(jnp.int32, part.shape, 0)
    part = jnp.where(row < 3, part_hi, jnp.where(row < 6, part_mid, part_lo)).astype(BF16)
    direct = dot(part, x_ref[...], ((1,), (0,)))
    pred_mine[...] = jnp.zeros_like(pred_mine)
    pred_mine[0:3, :] = direct[0:3] + direct[3:6] + direct[6:9]

    wide = 256

    def forward(group, now=True):
        def assemble(yy, carry):
            def tile(t):
                return wbuf[group, yy * SIDE + t // SHARE, t % SHARE]

            end = unpack_last(tile(10).astype(F32), tile(11).astype(F32), wext[group, yy].astype(F32))
            for band in range(BANDS):
                at = pl.ds(yy * rows + 16 * band, 16)
                wmat[group, at, 0:128] = tile(band)
                wmat[group, at, 128:256] = tile(BANDS + band)
                wmat[group, at, 256:384] = end[band].astype(BF16)
            return carry

        lax.fori_loop(0, SIDE, assemble, 0)
        head_t[group] = wmat[group, :, 256:384].astype(F32).T[HEAD : HEAD + 16].astype(BF16)

        def columns(n, carry):
            at = pl.ds(pl.multiple_of(n * wide, wide), wide)
            pre = dot(wmat[group], normed[:, at], ((1,), (0,)))
            sig = 0.5 * jnp.tanh(0.5 * pre) + 0.5
            act = pre * sig
            hid = act.astype(BF16)
            hidden[group, :, at] = hid
            slope[group, :, at] = sig + act * (1.0 - sig) if now else pre
            through = dot(head_t[group], hid, ((1,), (0,)))
            pred_mine[0:3, at] += through[0:3] + through[3:6]
            return carry

        lax.fori_loop(0, pixels // wide, columns, 0, unroll=True)

    def forward_on(k):
        group = (zh + SIDE - k) % SIDE
        if k == 2:
            relays[1].wait_recv()
            relays[3].wait_recv()
            when_mine(group, relay_ext.wait_recv)
        else:
            along_z[k].wait_recv()
            when_mine(group, along_z_ext[k].wait_recv)
            some = wbuf.at[group, here, pl.ds(0, 2) if k == 1 else pl.ds(2, 1)]
            relays[k] = remote(some, some, e_send.at[k], e_recv.at[k], group_peer(k))
            relays[k].start()
            if k == 3:
                when_mine(group, relay_ext.start)
        chunk = wbuf.at[group, here]
        extra = wext.at[group, y]

        def send(i, carry):
            remote(chunk, chunk, b_send.at[k], b_recv.at[k], plane_peer(i)).start()
            when_mine(group, remote(extra, extra, bx_send.at[k], bx_recv.at[k], plane_peer(i)).start)
            return carry

        lax.fori_loop(1, OTHERS + 1, send, 0)

    def wait_group(k):
        group = (zh + SIDE - k) % SIDE
        wait_bytes(wbuf.at[0, 0:OTHERS], b_recv.at[k])

        @pl.when(x == group)
        def _():
            wait_bytes(wext.at[0, 0 : SIDE - 1], bx_recv.at[k])

        @pl.when(x != group)
        def _():
            wait_bytes(wext.at[0], bx_recv.at[k])

    relays = {}
    passed = wext.at[(zh + 1) % SIDE, y]
    relay_ext = remote(passed, passed, ex_send, ex_recv, group_peer(3))
    for k in (1, 3):
        forward_on(k)
    for c in along_y:
        c.wait_recv()
    forward(zh)
    forward_on(2)
    samples = counts_ref[...].astype(F32)
    weight = samples / (samples + 64.0)
    g_rows[...] = jnp.zeros_like(g_rows)
    g_aug[...] = jnp.zeros_like(g_aug)
    for k in (1, 3, 2):
        wait_group(k)
        forward((zh + SIDE - k) % SIDE, now=k != 2)

    swap = remote(pred_mine, pred_other, p_send, p_recv, (1 - pair, dp, fsdp))
    swap.start()
    pred = pred_mine[0:3, :]
    for k in range(3):
        pred_ref[k] = pred[k : k + 1]
    toward = weight * (pred - target_ref[...])

    far = (zh + 2) % SIDE

    def make_slope(n, carry):
        at = pl.ds(pl.multiple_of(n * wide, wide), wide)
        pre = slope[far, :, at]
        sig = 0.5 * jnp.tanh(0.5 * pre) + 0.5
        slope[far, :, at] = sig + pre * sig * (1.0 - sig)
        return carry

    lax.fori_loop(0, pixels // wide, make_slope, 0)
    swap.wait_recv()
    g_pred = (toward + DISTILL * (pred - pred_other[0:3, :])) * loss_scale
    g_hi = g_pred.astype(BF16).astype(F32)
    g_rows[0:3, :] = g_hi
    g_rows[3:6, :] = g_hi
    g_rows[6:9, :] = g_pred - g_hi
    g_aug[HEAD : HEAD + 16, :] = g_rows[...].astype(BF16)

    def backward_rows(group, picks):
        ys = [(y + b) % SIDE for b in picks]

        def pick(ref, *rest):
            return jnp.concatenate([ref[(group, pl.ds(yy * rows, rows), *rest)] for yy in ys], axis=0)

        g_hidden = dot(pick(wmat, slice(256, 384)), g_aug[...], ((1,), (0,)))
        g_pre = (g_hidden * pick(slope, slice(None))).astype(BF16)
        grad = dot(g_pre, normed[...], ((1,), (1,)))
        for_head = dot(pick(hidden, slice(None)), g_aug[...], ((1,), (1,)))
        lane_g = lax.broadcasted_iota(jnp.int32, for_head.shape, 1)
        is_rest = (lane_g >= HEAD + 3) & (lane_g < HEAD + 6)
        for_head = jnp.where(is_rest, for_head - for_head.astype(BF16).astype(F32), for_head)
        for n, yy in enumerate(ys):
            at = slice(n * rows, n * rows + rows)
            tiles = pack(grad[at, 0:128], grad[at, 128:256], grad[at, 256:384])
            for t in range(TILES - 1):
                gsend[group, yy * SIDE + t // SHARE, t % SHARE] = tiles[t]
            gext[group, yy] = pack_end(grad[at, 256:384], for_head[at])

        for b in picks:
            yy = (y + b) % SIDE

            def send(a, carry):
                xx = (x + a) % SIDE
                remote(
                    gsend.at[group, yy * SIDE + xx], grecv.at[group, here],
                    r_send.at[group], r_recv.at[group], device(xx, yy, zh, zl),
                ).start()
                return carry

            lax.fori_loop(1 if b == 0 else 0, SIDE, send, 0)

    def backward(group, parts):
        for picks in parts:
            backward_rows(group, picks)
        grecv[group, here] = gsend[group, here]

        def send_ext(b, carry):
            to = (y + b) % SIDE
            remote(
                gext.at[group, to], xrecv.at[here], rx_send.at[group], rx_recv, device(group, to, zh, zl)
            ).start()
            return carry

        @pl.when(x == group)
        def _():
            lax.fori_loop(1, SIDE, send_ext, 0)
            xrecv[here] = gext[group, y]

        @pl.when(x != group)
        def _():
            lax.fori_loop(0, SIDE, send_ext, 0)

    order = [(zh + k) % SIDE for k in (2, 1, 3, 0)]

    def plane_sum(group):
        wait_bytes(grecv.at[0, 0:OTHERS], r_recv.at[group])
        total = grecv[group, 0].astype(F32)
        for s in range(1, SIDE * SIDE):
            total = total + grecv[group, s].astype(F32)
        zsend[group] = total

        own_slot = zrecv.at[zh * SIDE + zl]

        def send(to, carry):
            @pl.when((group != zh) | (to != zl))
            def _():
                remote(zsend.at[group, to], own_slot, z_send, z_recv, device(x, y, group, to)).start()

            return carry

        lax.fori_loop(0, SHARE, send, 0)

        @pl.when(x == group)
        def _():
            wait_bytes(xrecv.at[0:OTHERS], rx_recv)
            total = xrecv[0].astype(F32)
            for s in range(1, SIDE * SIDE):
                total = total + xrecv[s].astype(F32)
            zext[...] = total

            @pl.when((group != zh) | (zl != SHARE))
            def _():
                remote(zext, own_slot, z_send, z_recv, device(x, y, group, SHARE)).start()

    whole = (2, 1, 3, 0)
    for n, group in enumerate(order):
        backward(group, (whole[:2], whole[2:]) if n == 0 else (whole,))
    for group in order:
        plane_sum(group)
    has_tile = (zl < SHARE) | (x == zh)

    @pl.when(zl < SHARE)
    def _():
        zrecv[zh * SIDE + zl] = zsend[zh, zl]

    @pl.when((zl == SHARE) & (x == zh))
    def _():
        zrecv[zh * SIDE + zl] = zext[...]

    @pl.when(has_tile)
    def _():
        wait_bytes(zrecv.at[0:OTHERS], z_recv)
        total = zrecv[0]
        for s in range(1, SIDE * SIDE):
            total = total + zrecv[s]
        own = jnp.where(zl < SHARE, x * SHARE + zl, TILES - 1)
        fbuf[own] = total

        def send_piece(i, carry):
            remote(fbuf.at[own], fbuf.at[own], f_send, f_recv, dp_peer(i)).start()
            return carry

        lax.fori_loop(1, OTHERS + 1, send_piece, 0)

    for k in (1, 2, 3):
        group = (zh + SIDE - k) % SIDE
        if k != 2:
            along_z[k].wait_send()
            when_mine(zh, along_z_ext[k].wait_send)
            relays[k].wait_send()
        wait_bytes(wbuf.at[0, 0:OTHERS], b_send.at[k])
        when_mine(group, lambda: wait_bytes(xrecv.at[0:OTHERS], bx_send.at[k]))
    when_mine((zh + 1) % SIDE, relay_ext.wait_send)
    for c in along_y:
        c.wait_send()
    swap.wait_send()
    for group in range(SIDE):
        wait_bytes(gsend.at[0, 0:OTHERS], r_send.at[group])

        @pl.when(x == group)
        def _():
            wait_bytes(gext.at[0, 0 : SIDE - 1], rx_send.at[group])

        @pl.when(x != group)
        def _():
            wait_bytes(gext.at[0], rx_send.at[group])

    @pl.when(has_tile)
    def _():
        wait_bytes(fbuf.at[0 : TILES - 1], z_send)
        wait_bytes(fbuf.at[0 : TILES - 1], f_recv)
        wait_bytes(zrecv.at[0:OTHERS], f_send)

    @pl.when(jnp.logical_not(has_tile))
    def _():
        wait_bytes(fbuf, z_send)
        wait_bytes(fbuf, f_recv)

    sums_ref[...] = fbuf[...]


def results(sums_ref, pred_in_ref, w_rgb_ref, pred_ref, grad_in_ref, grad_down_ref):
    pred_ref[...] = pred_in_ref[...]
    end = unpack_last(sums_ref[10], sums_ref[11], sums_ref[12])
    for band in range(BANDS):
        at = slice(16 * band, 16 * band + 16)
        grad_in_ref[at, 0:128] = sums_ref[band]
        grad_in_ref[at, 128:256] = sums_ref[BANDS + band]
        grad_in_ref[at, 256:320] = end[band][:, 0:64]
        total = 0.0
        for k in range(3):
            weight = sum(end[band][:, at + k : at + k + 1] for at in range(HEAD, HEAD + PARTS, 3))
            total = total + weight * w_rgb_ref[k]
        grad_down_ref[16 * band : 16 * band + 16, :] = total


def on_device(loss_scale, features, level_gain, levels, w_in, w_down, w_rgb, target, counts):
    channels, pixels = features.shape[1:]
    rows = w_in.shape[1]
    all_rows = SIDE * SIDE * rows
    group_rows = SIDE * rows
    plane = SIDE * SIDE
    dma = pltpu.SemaphoreType.DMA
    vmem = pl.BlockSpec(memory_space=pltpu.VMEM)
    flops = 2 * all_rows * pixels * (2 * 384 + 3 * 128)
    colours = jnp.transpose(w_rgb, (1, 0, 2))
    pred, sums = pl.pallas_call(
        lambda *refs: kernel(loss_scale, *refs),
        out_shape=(
            jax.ShapeDtypeStruct((3, 1, pixels), F32),
            jax.ShapeDtypeStruct((TILES, *TILE), F32),
        ),
        in_specs=[pl.BlockSpec(memory_space=pl.ANY)] * 4 + [vmem] * 4,
        out_specs=(vmem, vmem),
        scratch_shapes=[
            pltpu.VMEM((channels, pixels), BF16),
            pltpu.VMEM(level_gain.shape, F32),
            pltpu.VMEM((rows, channels), BF16),
            pltpu.VMEM((rows, channels), BF16),
            dma((4,)),
            pltpu.VMEM((16, channels), F32),
            pltpu.VMEM((128, channels), BF16),
            pltpu.VMEM((384, pixels), BF16),
            pltpu.VMEM((SIDE, plane, SHARE, *TILE), BF16),
            pltpu.VMEM((SIDE, SIDE, *TILE), BF16),
            pltpu.VMEM((SIDE, group_rows, 384), BF16),
            pltpu.VMEM((SIDE, 16, group_rows), BF16),
            pltpu.VMEM((SIDE, group_rows, pixels), BF16),
            pltpu.VMEM((SIDE, group_rows, pixels), F32),
            pltpu.VMEM((8, pixels), F32),
            pltpu.VMEM((8, pixels), F32),
            pltpu.VMEM((16, pixels), F32),
            pltpu.VMEM((128, pixels), BF16),
            pltpu.VMEM((SIDE, plane, SHARE, *TILE), BF16),
            pltpu.VMEM((SIDE, SIDE, *TILE), BF16),
            pltpu.VMEM((SIDE, plane, SHARE, *TILE), BF16),
            pltpu.VMEM((plane, *TILE), BF16),
            pltpu.VMEM((SIDE, SHARE, *TILE), F32),
            pltpu.VMEM(TILE, F32),
            pltpu.VMEM((plane, *TILE), F32),
            pltpu.VMEM((TILES, *TILE), F32),
            dma((SIDE,)), dma((SIDE,)), dma, dma, dma((SIDE,)), dma((SIDE,)), dma((SIDE,)), dma((SIDE,)), dma((SIDE,)), dma,
            dma((SIDE,)), dma((SIDE,)), dma((SIDE,)), dma((SIDE,)),
            dma((SIDE,)), dma((SIDE,)), dma((SIDE,)), dma((SIDE,)), dma, dma,
            dma((SIDE,)), dma((SIDE,)), dma, dma, dma, dma,
        ],
        compiler_params=pltpu.CompilerParams(
            collective_id=0, has_side_effects=True, vmem_limit_bytes=56 * 2**20
        ),
        cost_estimate=pl.CostEstimate(flops=flops, bytes_accessed=2**21, transcendentals=all_rows * pixels),
    )(features[0], level_gain, w_in[0], w_down[0], levels[None], colours, target, counts[None])
    pred, grad_in, grad_down = pl.pallas_call(
        results,
        out_shape=(
            jax.ShapeDtypeStruct((3, 1, pixels), F32),
            jax.ShapeDtypeStruct((rows, channels), F32),
            jax.ShapeDtypeStruct((rows, channels), F32),
        ),
        in_specs=[vmem] * 3,
        out_specs=(vmem, vmem, vmem),
    )(sums, pred, colours)
    return jnp.transpose(pred, (1, 0, 2)), grad_in[None], grad_down[None]


def solution(mesh):
    in_specs = (
        P("pair", None, ("dp", "fsdp")),
        P(),
        P(),
        P("pair", "fsdp", None),
        P("pair", "fsdp", None),
        P("pair", None, None),
        P(None, ("dp", "fsdp")),
        P(("dp", "fsdp")),
    )
    out_specs = (P("pair", None, ("dp", "fsdp")), P("pair", "fsdp", None), P("pair", "fsdp", None))

    def whole(features, *rest):
        loss_scale = math.sqrt(features.shape[1] / features.shape[2])
        return jax.shard_map(
            lambda *args: on_device(loss_scale, *args),
            mesh=mesh, in_specs=in_specs, out_specs=out_specs, check_vma=False,
        )(features, *rest)

    return whole
```

```python
import math

import jax
import jax.numpy as jnp
from jax import lax
from jax.experimental import pallas as pl
from jax.experimental.pallas import tpu as pltpu
from jax.sharding import PartitionSpec as P

IMG_PIX = 4096
EPS = 1e-06
DISTILL = 1.0

MESH = pl.DeviceIdType.MESH
HIGH = lax.Precision.HIGHEST
BF16 = jnp.bfloat16
F32 = jnp.float32

SIDE = 4
OTHERS = SIDE * SIDE - 1
TILE = (16, 128)
BANDS = 5
HEAD = 64
PARTS = 9
SHARE = 3
TILES = SIDE * SHARE + 1


def pack(slab0, slab1, last):
    band = [slice(16 * b, 16 * b + 16) for b in range(BANDS)]
    tiles = [slab0[at] for at in band] + [slab1[at] for at in band]
    tiles.append(last[band[0]] + pltpu.roll(last[band[1]], 64, 1))
    tiles.append(last[band[2]] + pltpu.roll(last[band[3]], 64, 1))
    return [t.astype(BF16) for t in tiles]


def pack_end(last, head):
    band = [slice(16 * b, 16 * b + 16) for b in range(BANDS)]
    end = last[band[4]] + head[band[0]]
    for b in range(1, BANDS):
        end = end + pltpu.roll(head[band[b]], PARTS * b, 1)
    return end.astype(BF16)


def unpack_last(ten, eleven, end):
    lane = lax.broadcasted_iota(jnp.int32, TILE, 1)
    values = [ten, pltpu.roll(ten, 64, 1), eleven, pltpu.roll(eleven, 64, 1), end]
    heads = [end] + [pltpu.roll(end, 128 - PARTS * b, 1) for b in range(1, BANDS)]
    return [jnp.where(lane < HEAD, v, h) for v, h in zip(values, heads)]


def dot(left, right, dims, **kw):
    return lax.dot_general(left, right, (dims, ((), ())), preferred_element_type=F32, **kw)


def kernel(
    loss_scale,
    x_hbm, table_hbm, w_in_hbm, w_down_hbm, levels_ref, w_rgb_ref, target_ref, counts_ref,
    pred_ref, sums_ref,
    x_ref, table_ref, w_in_ref, w_down_ref, in_sem,
    rgb_rows, rgb_parts, normed, wbuf, wext, wmat, normed_t, hidden, slope, pred_mine, pred_other, g_rows, g_aug,
    gsend, gext, grecv, xrecv, zsend, zext, zrecv, fbuf,
    ax_send, ax_recv, ex_send, ex_recv, yx_send, yx_recv, bx_send, bx_recv, rx_send, rx_recv,
    a_send, a_recv, e_send, e_recv, y_send, y_recv, b_send, b_recv, c_recv, cx_recv, p_send, p_recv,
    r_send, r_recv, z_send, z_recv, f_send, f_recv,
):
    pair = lax.axis_index("pair")
    dp = lax.axis_index("dp")
    fsdp = lax.axis_index("fsdp")
    x, zl = dp // SIDE, dp % SIDE
    y, zh = fsdp // SIDE, fsdp % SIDE
    here = y * SIDE + x
    channels, pixels = x_ref.shape
    rows = w_in_ref.shape[0]

    def device(x_, y_, zh_, zl_):
        return (pair, x_ * SIDE + zl_, y_ * SIDE + zh_)

    def plane_peer(i):
        return device((x + i % SIDE) % SIDE, (y + i // SIDE) % SIDE, zh, zl)

    def z_peer(i):
        return device(x, y, (zh + i // SIDE) % SIDE, (zl + i % SIDE) % SIDE)

    def dp_peer(i):
        return device((x + i // SIDE) % SIDE, y, zh, (zl + i % SIDE) % SIDE)

    def group_peer(k):
        return device(x, y, (zh + k) % SIDE, zl)

    loads = {}
    for n, (src, dst) in enumerate(
        ((w_in_hbm, w_in_ref), (w_down_hbm, w_down_ref), (x_hbm, x_ref), (table_hbm, table_ref))
    ):
        loads[n] = pltpu.make_async_copy(src, dst, in_sem.at[n])
        loads[n].start()

    barrier = pltpu.get_barrier_semaphore()

    def greet(peer):
        pl.semaphore_signal(barrier, inc=1, device_id=peer, device_id_type=MESH)

    def greet_all(i, carry):
        greet(plane_peer(i))
        return carry

    lax.fori_loop(1, OTHERS + 1, greet_all, 0)
    for a in range(SIDE):
        for b in range(1, SIDE):
            greet(dp_peer(a * SIDE + b))
    for k in (1, 3):
        greet(group_peer(k))
    greet((1 - pair, dp, fsdp))

    loads[0].wait()
    w_own = w_in_ref[...]
    last = w_own[:, 256:320].astype(F32)
    last = jnp.concatenate([last, jnp.zeros((rows, 64), F32)], axis=1)
    tiles = pack(w_own[:, 0:128], w_own[:, 128:256], last)
    for t in range(TILES - 1):
        wbuf[zh, y * SIDE + t // SHARE, t % SHARE] = tiles[t]

    pl.semaphore_wait(barrier, OTHERS + 12 + 2 + 1)

    def remote(src, dst, send, recv, peer):
        return pltpu.make_async_remote_copy(
            src_ref=src, dst_ref=dst, send_sem=send, recv_sem=recv,
            device_id=peer, device_id_type=MESH,
        )

    def wait_bytes(ref, sem):
        pltpu.make_async_copy(ref, ref, sem).wait()

    quarter = wbuf.at[zh, here]
    along_z = {}
    for k in (1, 3):
        along_z[k] = remote(quarter, quarter, a_send.at[k], a_recv.at[k], group_peer(k))
        along_z[k].start()

    def when_mine(group, copy):
        @pl.when(x == group)
        def _():
            copy()

    block = wbuf.at[zh, pl.ds(y * SIDE, SIDE)]
    along_y = []
    for m in range(1, SIDE):
        c = remote(block, block, y_send.at[m], y_recv.at[m], device(x, (y + m) % SIDE, zh, zl))
        c.start()
        along_y.append(c)

    rgb_rows[...] = jnp.zeros_like(rgb_rows)
    for copy in range(3):
        for k in range(3):
            at = 3 * copy + k
            rgb_rows[at : at + 1, :] = w_rgb_ref[k]
    part = rgb_rows[...]
    part_hi = part.astype(BF16).astype(F32)
    part_mid = (part - part_hi).astype(BF16).astype(F32)
    part_lo = part - part_hi - part_mid
    rgb_parts[...] = jnp.zeros_like(rgb_parts)
    for n, p in enumerate((part_hi, part_mid, part_lo)):
        rgb_parts[HEAD + 16 * n : HEAD + 16 * n + 16, :] = p.astype(BF16)
    loads[1].wait()
    head = dot(w_down_ref[...], rgb_parts[...], ((1,), (1,)))
    head = head + pltpu.roll(head, 112, 1) + pltpu.roll(head, 96, 1)
    lane = lax.broadcasted_iota(jnp.int32, (rows, 128), 1)
    head = jnp.where((lane >= HEAD) & (lane < HEAD + PARTS), head, 0.0)
    head_hi = head.astype(BF16).astype(F32)
    is_lo = (lane >= HEAD + 3) & (lane < HEAD + 6)
    head = jnp.where(is_lo, head - head_hi, head_hi)
    own_ext = wext.at[zh, y]
    own_ext[...] = pack_end(last, head)
    along_z_ext = {}
    for k in (1, 3):
        along_z_ext[k] = remote(own_ext, own_ext, ax_send.at[k], ax_recv.at[k], group_peer(k))
        when_mine(zh, along_z_ext[k].start)
    for m in range(1, SIDE):
        peer = device(x, (y + m) % SIDE, zh, zl)
        c = remote(own_ext, own_ext, yx_send.at[m], yx_recv.at[m], peer)
        c.start()
        along_y.append(c)

    loads[2].wait()
    loads[3].wait()
    image = ((dp * SIDE * SIDE + fsdp) * pixels) // IMG_PIX
    levels = levels_ref[...].astype(F32)
    spots = lax.broadcasted_iota(jnp.int32, levels.shape, 1)
    level = jnp.sum(jnp.where(spots == image, levels, 0.0), axis=1, keepdims=True)
    table_rows = lax.broadcasted_iota(jnp.int32, table_ref.shape, 0).astype(F32)
    gain = jnp.sum(jnp.where(table_rows == level, table_ref[...], 0.0), axis=0, keepdims=True)
    gain = jnp.concatenate([gain, jnp.zeros((1, 384 - channels), F32)], axis=1)
    gain = jnp.broadcast_to(gain, (128, 384)).T[:channels, 0:1]
    xf = x_ref[...].astype(F32)
    mean_sq = jnp.mean(xf * xf, axis=0, keepdims=True)
    whole = xf * lax.rsqrt(mean_sq + EPS) * gain
    whole = jnp.concatenate([whole, jnp.zeros((384 - channels, pixels), F32)], axis=0)
    normed[...] = whole.astype(BF16)
    normed_t[...] = whole.T.astype(BF16)

    row = lax.broadcasted_iota(jnp.int32, part.shape, 0)
    part = jnp.where(row < 3, part_hi, jnp.where(row < 6, part_mid, part_lo)).astype(BF16)
    direct = dot(part, x_ref[...], ((1,), (0,)))
    pred_mine[...] = jnp.zeros_like(pred_mine)
    pred_mine[0:3, :] = direct[0:3] + direct[3:6] + direct[6:9]

    wide = 256

    def assemble(group, yy):
        def tile(t):
            return wbuf[group, yy * SIDE + t // SHARE, t % SHARE]

        end = unpack_last(tile(10).astype(F32), tile(11).astype(F32), wext[group, yy].astype(F32))
        for band in range(BANDS):
            at = pl.ds(yy * rows + 16 * band, 16)
            wmat[group, at, 0:128] = tile(band)
            wmat[group, at, 128:256] = tile(BANDS + band)
            wmat[group, at, 256:384] = end[band].astype(BF16)

    def sigmoid(pre):
        return 0.5 * jnp.tanh(0.5 * pre) + 0.5

    def forward(group):
        def assemble_one(yy, carry):
            assemble(group, yy)
            return carry

        lax.fori_loop(0, SIDE, assemble_one, 0)
        head_t = wmat[group, :, 256:384].astype(F32).T[HEAD : HEAD + 16].astype(BF16)
        for n in range(pixels // wide):
            at = slice(n * wide, n * wide + wide)
            pre = dot(wmat[group], normed[:, at], ((1,), (0,)))
            sig = sigmoid(pre)
            act = pre * sig
            hid = act.astype(BF16)
            hidden[group, :, at] = hid
            slope[group, :, at] = sig + act * (1.0 - sig)
            through = dot(head_t, hid, ((1,), (0,)))
            pred_mine[0:3, at] += through[0:3] + through[3:6]

    def forward_far(yy):
        assemble(far, yy)
        mine = pl.ds(yy * rows, rows)
        head_t = wmat[far, mine, 256:384].astype(F32).T[HEAD : HEAD + 16].astype(BF16)
        for n in range(pixels // wide):
            at = slice(n * wide, n * wide + wide)
            pre = dot(wmat[far, mine, :], normed[:, at], ((1,), (0,)))
            slope[far, mine, at] = pre
            hid = (pre * sigmoid(pre)).astype(BF16)
            hidden[far, mine, at] = hid
            through = dot(head_t, hid, ((1,), (0,)))
            pred_mine[0:3, at] += through[0:3] + through[3:6]

    relays = {}
    passed = wext.at[(zh + 1) % SIDE, y]
    relay_ext = remote(passed, passed, ex_send, ex_recv, group_peer(3))

    def relay(k):
        group = (zh + SIDE - k) % SIDE
        along_z[k].wait_recv()
        some = wbuf.at[group, here, pl.ds(0, 2) if k == 1 else pl.ds(2, 1)]
        relays[k] = remote(some, some, e_send.at[k], e_recv.at[k], group_peer(k))
        relays[k].start()
        when_mine(group, along_z_ext[k].wait_recv)
        if k == 3:
            when_mine(group, relay_ext.start)

    def forward_on(k):
        group = (zh + SIDE - k) % SIDE
        chunk = wbuf.at[group, here]
        extra = wext.at[group, y]

        def send(i, carry):
            remote(chunk, chunk, b_send.at[k], b_recv.at[k], plane_peer(i)).start()
            when_mine(group, remote(extra, extra, bx_send.at[k], bx_recv.at[k], plane_peer(i)).start)
            return carry

        lax.fori_loop(1, OTHERS + 1, send, 0)

    far = (zh + 2) % SIDE
    y_steps = (0, 1, 3, 2)

    def forward_far_on():
        relays[1].wait_recv()
        relays[3].wait_recv()
        when_mine(far, relay_ext.wait_recv)
        chunk = wbuf.at[far, here]
        extra = wext.at[far, y]
        for b in y_steps:

            def send(a, carry):
                peer = device((x + a) % SIDE, (y + b) % SIDE, zh, zl)
                remote(chunk, chunk, b_send.at[2], c_recv.at[b], peer).start()
                when_mine(far, remote(extra, extra, bx_send.at[2], cx_recv.at[b], peer).start)
                return carry

            lax.fori_loop(1 if b == 0 else 0, SIDE, send, 0)

    def wait_far(b):
        if b == 0:
            wait_bytes(wbuf.at[0, 0 : SIDE - 1], c_recv.at[b])

            @pl.when(x != far)
            def _():
                wait_bytes(wext.at[0, 0], cx_recv.at[b])
        else:
            wait_bytes(wbuf.at[0, 0:SIDE], c_recv.at[b])
            wait_bytes(wext.at[0, 0], cx_recv.at[b])

    def wait_group(k):
        group = (zh + SIDE - k) % SIDE
        wait_bytes(wbuf.at[0, 0:OTHERS], b_recv.at[k])

        @pl.when(x == group)
        def _():
            wait_bytes(wext.at[0, 0 : SIDE - 1], bx_recv.at[k])

        @pl.when(x != group)
        def _():
            wait_bytes(wext.at[0], bx_recv.at[k])

    for k in (1, 3):
        relay(k)
    for k in (1, 3):
        forward_on(k)
    for c in along_y:
        c.wait_recv()
    forward(zh)
    forward_far_on()
    samples = counts_ref[...].astype(F32)
    weight = samples / (samples + 64.0)
    g_rows[...] = jnp.zeros_like(g_rows)
    g_aug[...] = jnp.zeros_like(g_aug)
    for k in (1, 3):
        wait_group(k)
        forward((zh + SIDE - k) % SIDE)
    for b in y_steps:
        wait_far(b)
        forward_far((y + SIDE - b) % SIDE)

    swap = remote(pred_mine, pred_other, p_send, p_recv, (1 - pair, dp, fsdp))
    swap.start()
    pred = pred_mine[0:3, :]
    for k in range(3):
        pred_ref[k] = pred[k : k + 1]
    toward = weight * (pred - target_ref[...])

    def make_slope(n, carry):
        at = pl.ds(pl.multiple_of(n * wide, wide), wide)
        pre = slope[far, :, at]
        sig = sigmoid(pre)
        slope[far, :, at] = sig + pre * sig * (1.0 - sig)
        return carry

    lax.fori_loop(0, pixels // wide, make_slope, 0)
    swap.wait_recv()
    g_pred = (toward + DISTILL * (pred - pred_other[0:3, :])) * loss_scale
    g_hi = g_pred.astype(BF16).astype(F32)
    g_rows[0:3, :] = g_hi
    g_rows[3:6, :] = g_hi
    g_rows[6:9, :] = g_pred - g_hi
    g_aug[HEAD : HEAD + 16, :] = g_rows[...].astype(BF16)

    def backward_rows(group, picks):
        ys = [(y + b) % SIDE for b in picks]

        def pick(ref, *rest):
            return jnp.concatenate([ref[(group, pl.ds(yy * rows, rows), *rest)] for yy in ys], axis=0)

        g_hidden = dot(pick(wmat, slice(256, 384)), g_aug[...], ((1,), (0,)))
        g_pre = (g_hidden * pick(slope, slice(None))).astype(BF16)
        grad = dot(g_pre, normed_t[...], ((1,), (0,)))
        for_head = dot(pick(hidden, slice(None)), g_aug[...], ((1,), (1,)))
        lane_g = lax.broadcasted_iota(jnp.int32, for_head.shape, 1)
        is_rest = (lane_g >= HEAD + 3) & (lane_g < HEAD + 6)
        for_head = jnp.where(is_rest, for_head - for_head.astype(BF16).astype(F32), for_head)
        for n, yy in enumerate(ys):
            at = slice(n * rows, n * rows + rows)
            tiles = pack(grad[at, 0:128], grad[at, 128:256], grad[at, 256:384])
            for t in range(TILES - 1):
                gsend[group, yy * SIDE + t // SHARE, t % SHARE] = tiles[t]
            gext[group, yy] = pack_end(grad[at, 256:384], for_head[at])

        for b in picks:
            yy = (y + b) % SIDE

            def send(a, carry):
                xx = (x + a) % SIDE
                remote(
                    gsend.at[group, yy * SIDE + xx], grecv.at[group, here],
                    r_send.at[group], r_recv.at[group], device(xx, yy, zh, zl),
                ).start()
                return carry

            lax.fori_loop(1 if b == 0 else 0, SIDE, send, 0)

    def backward(group, parts):
        for picks in parts:
            backward_rows(group, picks)
        grecv[group, here] = gsend[group, here]

        def send_ext(b, carry):
            to = (y + b) % SIDE
            remote(
                gext.at[group, to], xrecv.at[here], rx_send.at[group], rx_recv, device(group, to, zh, zl)
            ).start()
            return carry

        @pl.when(x == group)
        def _():
            lax.fori_loop(1, SIDE, send_ext, 0)
            xrecv[here] = gext[group, y]

        @pl.when(x != group)
        def _():
            lax.fori_loop(0, SIDE, send_ext, 0)

    order = [(zh + k) % SIDE for k in (2, 1, 3, 0)]

    def plane_sum(group):
        wait_bytes(grecv.at[0, 0:OTHERS], r_recv.at[group])
        total = grecv[group, 0].astype(F32)
        for s in range(1, SIDE * SIDE):
            total = total + grecv[group, s].astype(F32)
        zsend[group] = total

        own_slot = zrecv.at[zh * SIDE + zl]

        def send(to, carry):
            @pl.when((group != zh) | (to != zl))
            def _():
                remote(zsend.at[group, to], own_slot, z_send, z_recv, device(x, y, group, to)).start()

            return carry

        lax.fori_loop(0, SHARE, send, 0)

        @pl.when(x == group)
        def _():
            wait_bytes(xrecv.at[0:OTHERS], rx_recv)
            total = xrecv[0].astype(F32)
            for s in range(1, SIDE * SIDE):
                total = total + xrecv[s].astype(F32)
            zext[...] = total

            @pl.when((group != zh) | (zl != SHARE))
            def _():
                remote(zext, own_slot, z_send, z_recv, device(x, y, group, SHARE)).start()

    for n, group in enumerate(order):
        backward(group, ((2,), (1,), (3, 0)) if n == 0 else ((2, 1, 3, 0),))
    for group in order:
        plane_sum(group)
    has_tile = (zl < SHARE) | (x == zh)

    @pl.when(zl < SHARE)
    def _():
        zrecv[zh * SIDE + zl] = zsend[zh, zl]

    @pl.when((zl == SHARE) & (x == zh))
    def _():
        zrecv[zh * SIDE + zl] = zext[...]

    @pl.when(has_tile)
    def _():
        wait_bytes(zrecv.at[0:OTHERS], z_recv)
        total = zrecv[0]
        for s in range(1, SIDE * SIDE):
            total = total + zrecv[s]
        own = jnp.where(zl < SHARE, x * SHARE + zl, TILES - 1)
        fbuf[own] = total

        def send_piece(i, carry):
            remote(fbuf.at[own], fbuf.at[own], f_send, f_recv, dp_peer(i)).start()
            return carry

        lax.fori_loop(1, OTHERS + 1, send_piece, 0)

    for k in (1, 2, 3):
        group = (zh + SIDE - k) % SIDE
        if k != 2:
            along_z[k].wait_send()
            when_mine(zh, along_z_ext[k].wait_send)
            relays[k].wait_send()
        wait_bytes(wbuf.at[0, 0:OTHERS], b_send.at[k])
        when_mine(group, lambda: wait_bytes(xrecv.at[0:OTHERS], bx_send.at[k]))
    when_mine((zh + 1) % SIDE, relay_ext.wait_send)
    for c in along_y:
        c.wait_send()
    swap.wait_send()
    for group in range(SIDE):
        wait_bytes(gsend.at[0, 0:OTHERS], r_send.at[group])

        @pl.when(x == group)
        def _():
            wait_bytes(gext.at[0, 0 : SIDE - 1], rx_send.at[group])

        @pl.when(x != group)
        def _():
            wait_bytes(gext.at[0], rx_send.at[group])

    @pl.when(has_tile)
    def _():
        wait_bytes(fbuf.at[0 : TILES - 1], z_send)
        wait_bytes(fbuf.at[0 : TILES - 1], f_recv)
        wait_bytes(zrecv.at[0:OTHERS], f_send)

    @pl.when(jnp.logical_not(has_tile))
    def _():
        wait_bytes(fbuf, z_send)
        wait_bytes(fbuf, f_recv)

    sums_ref[...] = fbuf[...]


def results(sums_ref, pred_in_ref, w_rgb_ref, pred_ref, grad_in_ref, grad_down_ref):
    pred_ref[...] = pred_in_ref[...]
    end = unpack_last(sums_ref[10], sums_ref[11], sums_ref[12])
    for band in range(BANDS):
        at = slice(16 * band, 16 * band + 16)
        grad_in_ref[at, 0:128] = sums_ref[band]
        grad_in_ref[at, 128:256] = sums_ref[BANDS + band]
        grad_in_ref[at, 256:320] = end[band][:, 0:64]
        total = 0.0
        for k in range(3):
            weight = sum(end[band][:, at + k : at + k + 1] for at in range(HEAD, HEAD + PARTS, 3))
            total = total + weight * w_rgb_ref[k]
        grad_down_ref[16 * band : 16 * band + 16, :] = total


def on_device(loss_scale, features, level_gain, levels, w_in, w_down, w_rgb, target, counts):
    channels, pixels = features.shape[1:]
    rows = w_in.shape[1]
    all_rows = SIDE * SIDE * rows
    group_rows = SIDE * rows
    plane = SIDE * SIDE
    dma = pltpu.SemaphoreType.DMA
    vmem = pl.BlockSpec(memory_space=pltpu.VMEM)
    flops = 2 * all_rows * pixels * (2 * 384 + 3 * 128)
    colours = jnp.transpose(w_rgb, (1, 0, 2))
    pred, sums = pl.pallas_call(
        lambda *refs: kernel(loss_scale, *refs),
        out_shape=(
            pltpu.VMEM((3, 1, pixels), F32),
            pltpu.VMEM((TILES, *TILE), F32),
        ),
        in_specs=[pl.BlockSpec(memory_space=pl.ANY)] * 4 + [vmem] * 4,
        out_specs=(vmem, vmem),
        scratch_shapes=[
            pltpu.VMEM((channels, pixels), BF16),
            pltpu.VMEM(level_gain.shape, F32),
            pltpu.VMEM((rows, channels), BF16),
            pltpu.VMEM((rows, channels), BF16),
            dma((4,)),
            pltpu.VMEM((16, channels), F32),
            pltpu.VMEM((128, channels), BF16),
            pltpu.VMEM((384, pixels), BF16),
            pltpu.VMEM((SIDE, plane, SHARE, *TILE), BF16),
            pltpu.VMEM((SIDE, SIDE, *TILE), BF16),
            pltpu.VMEM((SIDE, group_rows, 384), BF16),
            pltpu.VMEM((pixels, 384), BF16),
            pltpu.VMEM((SIDE, group_rows, pixels), BF16),
            pltpu.VMEM((SIDE, group_rows, pixels), F32),
            pltpu.VMEM((8, pixels), F32),
            pltpu.VMEM((8, pixels), F32),
            pltpu.VMEM((16, pixels), F32),
            pltpu.VMEM((128, pixels), BF16),
            pltpu.VMEM((SIDE, plane, SHARE, *TILE), BF16),
            pltpu.VMEM((SIDE, SIDE, *TILE), BF16),
            pltpu.VMEM((SIDE, plane, SHARE, *TILE), BF16),
            pltpu.VMEM((plane, *TILE), BF16),
            pltpu.VMEM((SIDE, SHARE, *TILE), F32),
            pltpu.VMEM(TILE, F32),
            pltpu.VMEM((plane, *TILE), F32),
            pltpu.VMEM((TILES, *TILE), F32),
            dma((SIDE,)), dma((SIDE,)), dma, dma, dma((SIDE,)), dma((SIDE,)), dma((SIDE,)), dma((SIDE,)), dma((SIDE,)), dma,
            dma((SIDE,)), dma((SIDE,)), dma((SIDE,)), dma((SIDE,)),
            dma((SIDE,)), dma((SIDE,)), dma((SIDE,)), dma((SIDE,)), dma((SIDE,)), dma((SIDE,)), dma, dma,
            dma((SIDE,)), dma((SIDE,)), dma, dma, dma, dma,
        ],
        compiler_params=pltpu.CompilerParams(
            collective_id=0, has_side_effects=True, vmem_limit_bytes=56 * 2**20
        ),
        cost_estimate=pl.CostEstimate(flops=flops, bytes_accessed=2**21, transcendentals=all_rows * pixels),
    )(features[0], level_gain, w_in[0], w_down[0], levels[None], colours, target, counts[None])
    pred, grad_in, grad_down = pl.pallas_call(
        results,
        out_shape=(
            jax.ShapeDtypeStruct((3, 1, pixels), F32),
            jax.ShapeDtypeStruct((rows, channels), F32),
            jax.ShapeDtypeStruct((rows, channels), F32),
        ),
        in_specs=[vmem] * 3,
        out_specs=(vmem, vmem, vmem),
    )(sums, pred, colours)
    return jnp.transpose(pred, (1, 0, 2)), grad_in[None], grad_down[None]


def solution(mesh):
    in_specs = (
        P("pair", None, ("dp", "fsdp")),
        P(),
        P(),
        P("pair", "fsdp", None),
        P("pair", "fsdp", None),
        P("pair", None, None),
        P(None, ("dp", "fsdp")),
        P(("dp", "fsdp")),
    )
    out_specs = (P("pair", None, ("dp", "fsdp")), P("pair", "fsdp", None), P("pair", "fsdp", None))

    def whole(features, *rest):
        loss_scale = math.sqrt(features.shape[1] / features.shape[2])
        return jax.shard_map(
            lambda *args: on_device(loss_scale, *args),
            mesh=mesh, in_specs=in_specs, out_specs=out_specs, check_vma=False,
        )(features, *rest)

    return whole
```

```python
import math

import jax
import jax.numpy as jnp
from jax import lax
from jax.experimental import pallas as pl
from jax.experimental.pallas import tpu as pltpu
from jax.sharding import PartitionSpec as P

IMG_PIX = 4096
EPS = 1e-06
DISTILL = 1.0

MESH = pl.DeviceIdType.MESH
HIGH = lax.Precision.HIGHEST
BF16 = jnp.bfloat16
F32 = jnp.float32

SIDE = 4
OTHERS = SIDE * SIDE - 1
TILE = (16, 128)
BANDS = 5
HEAD = 64
PARTS = 9
SHARE = 3
TILES = SIDE * SHARE + 1


def pack(slab0, slab1, last):
    band = [slice(16 * b, 16 * b + 16) for b in range(BANDS)]
    tiles = [slab0[at] for at in band] + [slab1[at] for at in band]
    tiles.append(last[band[0]] + pltpu.roll(last[band[1]], 64, 1))
    tiles.append(last[band[2]] + pltpu.roll(last[band[3]], 64, 1))
    return [t.astype(BF16) for t in tiles]


def pack_end(last, head):
    band = [slice(16 * b, 16 * b + 16) for b in range(BANDS)]
    end = last[band[4]] + head[band[0]]
    for b in range(1, BANDS):
        end = end + pltpu.roll(head[band[b]], PARTS * b, 1)
    return end.astype(BF16)


def unpack_last(ten, eleven, end):
    lane = lax.broadcasted_iota(jnp.int32, TILE, 1)
    values = [ten, pltpu.roll(ten, 64, 1), eleven, pltpu.roll(eleven, 64, 1), end]
    heads = [end] + [pltpu.roll(end, 128 - PARTS * b, 1) for b in range(1, BANDS)]
    return [jnp.where(lane < HEAD, v, h) for v, h in zip(values, heads)]


def dot(left, right, dims, **kw):
    return lax.dot_general(left, right, (dims, ((), ())), preferred_element_type=F32, **kw)


def kernel(
    loss_scale,
    x_hbm, table_hbm, w_in_hbm, w_down_hbm, levels_ref, w_rgb_ref, target_ref, counts_ref,
    pred_ref, sums_ref,
    x_ref, table_ref, w_in_ref, w_down_ref, in_sem,
    rgb_rows, rgb_parts, normed, wbuf, wext, wmat, head_t, hidden, slope, pred_mine, pred_other, g_rows, g_aug,
    gsend, gext, grecv, xrecv, zsend, zext, zrecv, fbuf,
    ax_send, ax_recv, ex_send, ex_recv, yx_send, yx_recv, bx_send, bx_recv, rx_send, rx_recv,
    a_send, a_recv, e_send, e_recv, y_send, y_recv, b_send, b_recv, p_send, p_recv,
    r_send, r_recv, z_send, z_recv, f_send, f_recv,
):
    pair = lax.axis_index("pair")
    dp = lax.axis_index("dp")
    fsdp = lax.axis_index("fsdp")
    x, zl = lax.div(dp, SIDE), lax.rem(dp, SIDE)
    y, zh = lax.div(fsdp, SIDE), lax.rem(fsdp, SIDE)
    xs, ys, zls, zhs = ([at] + [lax.rem(at + n, SIDE) for n in range(1, SIDE)] for at in (x, y, zl, zh))
    steps = (2, 1, 3, 0)
    around = [(a, b) for b in steps for a in steps if (a, b) != (0, 0)]
    here = y * SIDE + x
    channels, pixels = x_ref.shape
    rows = w_in_ref.shape[0]

    def device(x_, y_, zh_, zl_):
        return (pair, x_ * SIDE + zl_, y_ * SIDE + zh_)

    def plane_peer(a, b):
        return device(xs[a], ys[b], zh, zl)

    def dp_peer(a, b):
        return device(xs[a], y, zh, zls[b])

    def group_peer(k):
        return device(x, y, zhs[k], zl)

    barrier = pltpu.get_barrier_semaphore()

    def greet(peer):
        pl.semaphore_signal(barrier, inc=1, device_id=peer, device_id_type=MESH)

    for k in (1, 3):
        greet(group_peer(k))
    loads = {}
    for n, (src, dst) in enumerate(
        ((w_in_hbm, w_in_ref), (w_down_hbm, w_down_ref), (x_hbm, x_ref), (table_hbm, table_ref))
    ):
        loads[n] = pltpu.make_async_copy(src, dst, in_sem.at[n])
        loads[n].start()
    for a, b in around:
        greet(plane_peer(a, b))
        if b:
            greet(dp_peer(a, b))
    greet((1 - pair, dp, fsdp))
    loads[0].wait()
    w_own = w_in_ref[...]
    last = w_own[:, 256:320].astype(F32)
    last = jnp.concatenate([last, jnp.zeros((rows, 64), F32)], axis=1)
    tiles = pack(w_own[:, 0:128], w_own[:, 128:256], last)
    for t in range(TILES - 1):
        wbuf[zh, y * SIDE + t // SHARE, t % SHARE] = tiles[t]

    pl.semaphore_wait(barrier, OTHERS + 12 + 2 + 1)

    def remote(src, dst, send, recv, peer):
        return pltpu.make_async_remote_copy(
            src_ref=src, dst_ref=dst, send_sem=send, recv_sem=recv,
            device_id=peer, device_id_type=MESH,
        )

    def wait_bytes(ref, sem):
        pltpu.make_async_copy(ref, ref, sem).wait()

    quarter = wbuf.at[zh, here]
    along_z = {}
    for k in (1, 3):
        along_z[k] = remote(quarter, quarter, a_send.at[k], a_recv.at[k], group_peer(k))
        along_z[k].start()

    def when_mine(group, copy):
        @pl.when(x == group)
        def _():
            copy()

    block = wbuf.at[zh, pl.ds(y * SIDE, SIDE)]
    along_y = []
    for m in range(1, SIDE):
        c = remote(block, block, y_send.at[m], y_recv.at[m], plane_peer(0, m))
        c.start()
        along_y.append(c)

    rgb_rows[...] = jnp.zeros_like(rgb_rows)
    for copy in range(3):
        for k in range(3):
            at = 3 * copy + k
            rgb_rows[at : at + 1, :] = w_rgb_ref[k]
    part = rgb_rows[...]
    part_hi = part.astype(BF16).astype(F32)
    part_mid = (part - part_hi).astype(BF16).astype(F32)
    part_lo = part - part_hi - part_mid
    rgb_parts[...] = jnp.zeros_like(rgb_parts)
    for n, p in enumerate((part_hi, part_mid, part_lo)):
        rgb_parts[HEAD + 16 * n : HEAD + 16 * n + 16, :] = p.astype(BF16)
    loads[1].wait()
    head = dot(w_down_ref[...], rgb_parts[...], ((1,), (1,)))
    head = head + pltpu.roll(head, 112, 1) + pltpu.roll(head, 96, 1)
    lane = lax.broadcasted_iota(jnp.int32, (rows, 128), 1)
    head = jnp.where((lane >= HEAD) & (lane < HEAD + PARTS), head, 0.0)
    head_hi = head.astype(BF16).astype(F32)
    is_lo = (lane >= HEAD + 3) & (lane < HEAD + 6)
    head = jnp.where(is_lo, head - head_hi, head_hi)
    own_ext = wext.at[zh, y]
    own_ext[...] = pack_end(last, head)
    along_z_ext = {}
    for k in (1, 3):
        along_z_ext[k] = remote(own_ext, own_ext, ax_send.at[k], ax_recv.at[k], group_peer(k))
        when_mine(zh, along_z_ext[k].start)
    for m in range(1, SIDE):
        c = remote(own_ext, own_ext, yx_send.at[m], yx_recv.at[m], plane_peer(0, m))
        c.start()
        along_y.append(c)

    loads[2].wait()
    loads[3].wait()
    image = ((dp * SIDE * SIDE + fsdp) * pixels) // IMG_PIX
    levels = levels_ref[...].astype(F32)
    spots = lax.broadcasted_iota(jnp.int32, levels.shape, 1)
    level = jnp.sum(jnp.where(spots == image, levels, 0.0), axis=1, keepdims=True)
    table_rows = lax.broadcasted_iota(jnp.int32, table_ref.shape, 0).astype(F32)
    gain = jnp.sum(jnp.where(table_rows == level, table_ref[...], 0.0), axis=0, keepdims=True)
    gain = jnp.concatenate([gain, jnp.zeros((1, 384 - channels), F32)], axis=1)
    gain = jnp.broadcast_to(gain, (128, 384)).T[:channels, 0:1]
    xf = x_ref[...].astype(F32)
    mean_sq = jnp.mean(xf * xf, axis=0, keepdims=True)
    whole = xf * lax.rsqrt(mean_sq + EPS) * gain
    whole = jnp.concatenate([whole, jnp.zeros((384 - channels, pixels), F32)], axis=0)
    normed[...] = whole.astype(BF16)

    row = lax.broadcasted_iota(jnp.int32, part.shape, 0)
    part = jnp.where(row < 3, part_hi, jnp.where(row < 6, part_mid, part_lo)).astype(BF16)
    direct = dot(part, x_ref[...], ((1,), (0,)))
    pred_mine[...] = jnp.zeros_like(pred_mine)
    pred_mine[0:3, :] = direct[0:3] + direct[3:6] + direct[6:9]

    wide = 512

    def assemble(group, yy):
        def tile(t):
            return wbuf[group, yy * SIDE + t // SHARE, t % SHARE]

        end = unpack_last(tile(10).astype(F32), tile(11).astype(F32), wext[group, yy].astype(F32))
        for band in range(BANDS):
            at = pl.ds(yy * rows + 16 * band, 16)
            wmat[group, at, 0:128] = tile(band)
            wmat[group, at, 128:256] = tile(BANDS + band)
            wmat[group, at, 256:384] = end[band].astype(BF16)

    def sigmoid(pre):
        return 0.5 * jnp.tanh(0.5 * pre) + 0.5

    def forward(group, now=True):
        def assemble_one(yy, carry):
            assemble(group, yy)
            return carry

        lax.fori_loop(0, SIDE, assemble_one, 0)
        head_t[group] = wmat[group, :, 256:384].astype(F32).T[HEAD : HEAD + 16].astype(BF16)

        def columns(n, carry):
            at = pl.ds(pl.multiple_of(n * wide, wide), wide)
            pre = dot(wmat[group], normed[:, at], ((1,), (0,)))
            sig = sigmoid(pre)
            act = pre * sig
            hid = act.astype(BF16)
            hidden[group, :, at] = hid
            slope[group, :, at] = sig + act * (1.0 - sig) if now else pre
            through = dot(head_t[group], hid, ((1,), (0,)))
            pred_mine[0:3, at] += through[0:3] + through[3:6]
            return carry

        lax.fori_loop(0, pixels // wide, columns, 0, unroll=True)

    relays = {}
    passed = wext.at[zhs[1], y]
    relay_ext = remote(passed, passed, ex_send, ex_recv, group_peer(3))

    def relay(k):
        group = zhs[-k]
        along_z[k].wait_recv()
        some = wbuf.at[group, here, pl.ds(0, 2) if k == 1 else pl.ds(2, 1)]
        relays[k] = remote(some, some, e_send.at[k], e_recv.at[k], group_peer(k))
        relays[k].start()
        when_mine(group, along_z_ext[k].wait_recv)
        if k == 3:
            when_mine(group, relay_ext.start)

    def forward_on(k):
        group = zhs[-k]
        if k == 2:
            relays[1].wait_recv()
            relays[3].wait_recv()
            when_mine(group, relay_ext.wait_recv)
        chunk = wbuf.at[group, here]
        extra = wext.at[group, y]

        for a, b in around:
            remote(chunk, chunk, b_send.at[k], b_recv.at[k], plane_peer(a, b)).start()

        @pl.when(x == group)
        def _():
            for a, b in around:
                remote(extra, extra, bx_send.at[k], bx_recv.at[k], plane_peer(a, b)).start()

    far = zhs[2]
    def wait_group(k):
        group = zhs[-k]
        wait_bytes(wbuf.at[0, 0:OTHERS], b_recv.at[k])

        @pl.when(x == group)
        def _():
            wait_bytes(wext.at[0, 0 : SIDE - 1], bx_recv.at[k])

        @pl.when(x != group)
        def _():
            wait_bytes(wext.at[0], bx_recv.at[k])

    for k in (1, 3):
        relay(k)
        forward_on(k)
    for c in along_y:
        c.wait_recv()
    forward(zh)
    forward_on(2)
    samples = counts_ref[...].astype(F32)
    weight = samples / (samples + 64.0)
    g_rows[...] = jnp.zeros_like(g_rows)
    g_aug[...] = jnp.zeros_like(g_aug)
    for k in (1, 3):
        wait_group(k)
        forward(zhs[-k])
    wait_group(2)
    forward(far, now=False)

    swap = remote(pred_mine, pred_other, p_send, p_recv, (1 - pair, dp, fsdp))
    swap.start()
    pred = pred_mine[0:3, :]
    for k in range(3):
        pred_ref[k] = pred[k : k + 1]
    toward = weight * (pred - target_ref[...])

    def make_slope(n, carry):
        at = pl.ds(pl.multiple_of(n * wide, wide), wide)
        pre = slope[far, :, at]
        sig = sigmoid(pre)
        slope[far, :, at] = sig + pre * sig * (1.0 - sig)
        return carry

    lax.fori_loop(0, pixels // wide, make_slope, 0)
    swap.wait_recv()
    g_pred = (toward + DISTILL * (pred - pred_other[0:3, :])) * loss_scale
    g_hi = g_pred.astype(BF16).astype(F32)
    g_rows[0:3, :] = g_hi
    g_rows[3:6, :] = g_hi
    g_rows[6:9, :] = g_pred - g_hi
    g_aug[HEAD : HEAD + 16, :] = g_rows[...].astype(BF16)

    def backward_rows(group, picks):
        owners = [ys[b] for b in picks]

        def pick(ref, *rest):
            return jnp.concatenate([ref[(group, pl.ds(yy * rows, rows), *rest)] for yy in owners], axis=0)

        g_hidden = dot(pick(wmat, slice(256, 384)), g_aug[...], ((1,), (0,)))
        g_pre = (g_hidden * pick(slope, slice(None))).astype(BF16)
        grad = dot(g_pre, normed[...], ((1,), (1,)))
        for_head = dot(pick(hidden, slice(None)), g_aug[...], ((1,), (1,)))
        lane_g = lax.broadcasted_iota(jnp.int32, for_head.shape, 1)
        is_rest = (lane_g >= HEAD + 3) & (lane_g < HEAD + 6)
        for_head = jnp.where(is_rest, for_head - for_head.astype(BF16).astype(F32), for_head)
        for n, yy in enumerate(owners):
            at = slice(n * rows, n * rows + rows)
            tiles = pack(grad[at, 0:128], grad[at, 128:256], grad[at, 256:384])
            for t in range(TILES - 1):
                gsend[group, yy * SIDE + t // SHARE, t % SHARE] = tiles[t]
            gext[group, yy] = pack_end(grad[at, 256:384], for_head[at])

        for a, b in around:
            if b in picks:
                remote(
                    gsend.at[group, ys[b] * SIDE + xs[a]], grecv.at[group, here],
                    r_send.at[group], r_recv.at[group], plane_peer(a, b),
                ).start()

    def backward(group, parts):
        for picks in parts:
            backward_rows(group, picks)
        grecv[group, here] = gsend[group, here]

        def send_ext(b):
            remote(
                gext.at[group, ys[b]], xrecv.at[here], rx_send.at[group], rx_recv, device(group, ys[b], zh, zl)
            ).start()

        for b in (2, 1, 3):
            send_ext(b)

        @pl.when(x == group)
        def _():
            xrecv[here] = gext[group, y]

        @pl.when(x != group)
        def _():
            send_ext(0)

    order = [zhs[k] for k in steps]

    def plane_sum(group, own):
        wait_bytes(grecv.at[0, 0:OTHERS], r_recv.at[group])
        total = grecv[group, 0].astype(F32)
        for s in range(1, SIDE * SIDE):
            total = total + grecv[group, s].astype(F32)
        zsend[group] = total

        own_slot = zrecv.at[zh * SIDE + zl]

        for to in range(SHARE):
            piece = remote(zsend.at[group, to], own_slot, z_send, z_recv, device(x, y, group, to))
            if own:
                pl.when(to != zl)(piece.start)
            else:
                piece.start()

        @pl.when(x == group)
        def _():
            wait_bytes(xrecv.at[0:OTHERS], rx_recv)
            total = xrecv[0].astype(F32)
            for s in range(1, SIDE * SIDE):
                total = total + xrecv[s].astype(F32)
            zext[...] = total

            piece = remote(zext, own_slot, z_send, z_recv, device(x, y, group, SHARE))
            if own:
                pl.when(zl != SHARE)(piece.start)
            else:
                piece.start()

    for n, group in enumerate(order):
        backward(group, ((2, 1), (3, 0)) if n == 0 else ((2, 1, 3, 0),))
    for k, group in zip(steps, order):
        plane_sum(group, k == 0)
    has_tile = (zl < SHARE) | (x == zh)

    @pl.when(zl < SHARE)
    def _():
        zrecv[zh * SIDE + zl] = zsend[zh, zl]

    @pl.when((zl == SHARE) & (x == zh))
    def _():
        zrecv[zh * SIDE + zl] = zext[...]

    @pl.when(has_tile)
    def _():
        wait_bytes(zrecv.at[0:OTHERS], z_recv)
        total = zrecv[0]
        for s in range(1, SIDE * SIDE):
            total = total + zrecv[s]
        own = jnp.where(zl < SHARE, x * SHARE + zl, TILES - 1)
        fbuf[own] = total

        for a, b in around:
            remote(fbuf.at[own], fbuf.at[own], f_send, f_recv, dp_peer(a, b)).start()

    for k in (1, 2, 3):
        group = zhs[-k]
        if k != 2:
            along_z[k].wait_send()
            when_mine(zh, along_z_ext[k].wait_send)
            relays[k].wait_send()
        wait_bytes(wbuf.at[0, 0:OTHERS], b_send.at[k])
        when_mine(group, lambda: wait_bytes(xrecv.at[0:OTHERS], bx_send.at[k]))
    when_mine(zhs[1], relay_ext.wait_send)
    for c in along_y:
        c.wait_send()
    swap.wait_send()
    for group in range(SIDE):
        wait_bytes(gsend.at[0, 0:OTHERS], r_send.at[group])

        @pl.when(x == group)
        def _():
            wait_bytes(gext.at[0, 0 : SIDE - 1], rx_send.at[group])

        @pl.when(x != group)
        def _():
            wait_bytes(gext.at[0], rx_send.at[group])

    @pl.when(has_tile)
    def _():
        wait_bytes(fbuf.at[0 : TILES - 1], z_send)
        wait_bytes(fbuf.at[0 : TILES - 1], f_recv)
        wait_bytes(zrecv.at[0:OTHERS], f_send)

    @pl.when(jnp.logical_not(has_tile))
    def _():
        wait_bytes(fbuf, z_send)
        wait_bytes(fbuf, f_recv)

    sums_ref[...] = fbuf[...]


def results(sums_ref, pred_in_ref, w_rgb_ref, pred_ref, grad_in_ref, grad_down_ref):
    pred_ref[...] = pred_in_ref[...]
    end = unpack_last(sums_ref[10], sums_ref[11], sums_ref[12])
    for band in range(BANDS):
        at = slice(16 * band, 16 * band + 16)
        grad_in_ref[at, 0:128] = sums_ref[band]
        grad_in_ref[at, 128:256] = sums_ref[BANDS + band]
        grad_in_ref[at, 256:320] = end[band][:, 0:64]
        total = 0.0
        for k in range(3):
            weight = sum(end[band][:, at + k : at + k + 1] for at in range(HEAD, HEAD + PARTS, 3))
            total = total + weight * w_rgb_ref[k]
        grad_down_ref[16 * band : 16 * band + 16, :] = total


def on_device(loss_scale, features, level_gain, levels, w_in, w_down, w_rgb, target, counts):
    channels, pixels = features.shape[1:]
    rows = w_in.shape[1]
    all_rows = SIDE * SIDE * rows
    group_rows = SIDE * rows
    plane = SIDE * SIDE
    dma = pltpu.SemaphoreType.DMA
    vmem = pl.BlockSpec(memory_space=pltpu.VMEM)
    flops = 2 * all_rows * pixels * (2 * 384 + 3 * 128)
    colours = jnp.transpose(w_rgb, (1, 0, 2))
    pred, sums = pl.pallas_call(
        lambda *refs: kernel(loss_scale, *refs),
        out_shape=(
            jax.ShapeDtypeStruct((3, 1, pixels), F32),
            jax.ShapeDtypeStruct((TILES, *TILE), F32),
        ),
        in_specs=[pl.BlockSpec(memory_space=pl.ANY)] * 4 + [vmem] * 4,
        out_specs=(vmem, vmem),
        scratch_shapes=[
            pltpu.VMEM((channels, pixels), BF16),
            pltpu.VMEM(level_gain.shape, F32),
            pltpu.VMEM((rows, channels), BF16),
            pltpu.VMEM((rows, channels), BF16),
            dma((4,)),
            pltpu.VMEM((16, channels), F32),
            pltpu.VMEM((128, channels), BF16),
            pltpu.VMEM((384, pixels), BF16),
            pltpu.VMEM((SIDE, plane, SHARE, *TILE), BF16),
            pltpu.VMEM((SIDE, SIDE, *TILE), BF16),
            pltpu.VMEM((SIDE, group_rows, 384), BF16),
            pltpu.VMEM((SIDE, 16, group_rows), BF16),
            pltpu.VMEM((SIDE, group_rows, pixels), BF16),
            pltpu.VMEM((SIDE, group_rows, pixels), F32),
            pltpu.VMEM((8, pixels), F32),
            pltpu.VMEM((8, pixels), F32),
            pltpu.VMEM((16, pixels), F32),
            pltpu.VMEM((128, pixels), BF16),
            pltpu.VMEM((SIDE, plane, SHARE, *TILE), BF16),
            pltpu.VMEM((SIDE, SIDE, *TILE), BF16),
            pltpu.VMEM((SIDE, plane, SHARE, *TILE), BF16),
            pltpu.VMEM((plane, *TILE), BF16),
            pltpu.VMEM((SIDE, SHARE, *TILE), F32),
            pltpu.VMEM(TILE, F32),
            pltpu.VMEM((plane, *TILE), F32),
            pltpu.VMEM((TILES, *TILE), F32),
            dma((SIDE,)), dma((SIDE,)), dma, dma, dma((SIDE,)), dma((SIDE,)), dma((SIDE,)), dma((SIDE,)), dma((SIDE,)), dma,
            dma((SIDE,)), dma((SIDE,)), dma((SIDE,)), dma((SIDE,)),
            dma((SIDE,)), dma((SIDE,)), dma((SIDE,)), dma((SIDE,)), dma, dma,
            dma((SIDE,)), dma((SIDE,)), dma, dma, dma, dma,
        ],
        compiler_params=pltpu.CompilerParams(
            collective_id=0, has_side_effects=True, vmem_limit_bytes=56 * 2**20
        ),
        cost_estimate=pl.CostEstimate(flops=flops, bytes_accessed=2**21, transcendentals=all_rows * pixels),
    )(features[0], level_gain, w_in[0], w_down[0], levels[None], colours, target, counts[None])
    pred, grad_in, grad_down = pl.pallas_call(
        results,
        out_shape=(
            jax.ShapeDtypeStruct((3, 1, pixels), F32),
            jax.ShapeDtypeStruct((rows, channels), F32),
            jax.ShapeDtypeStruct((rows, channels), F32),
        ),
        in_specs=[vmem] * 3,
        out_specs=(vmem, vmem, vmem),
    )(sums, pred, colours)
    return jnp.transpose(pred, (1, 0, 2)), grad_in[None], grad_down[None]


def solution(mesh):
    in_specs = (
        P("pair", None, ("dp", "fsdp")),
        P(),
        P(),
        P("pair", "fsdp", None),
        P("pair", "fsdp", None),
        P("pair", None, None),
        P(None, ("dp", "fsdp")),
        P(("dp", "fsdp")),
    )
    out_specs = (P("pair", None, ("dp", "fsdp")), P("pair", "fsdp", None), P("pair", "fsdp", None))

    def whole(features, *rest):
        loss_scale = math.sqrt(features.shape[1] / features.shape[2])
        return jax.shard_map(
            lambda *args: on_device(loss_scale, *args),
            mesh=mesh, in_specs=in_specs, out_specs=out_specs, check_vma=False,
        )(features, *rest)

    return whole
```

```python
import math

import jax
import jax.numpy as jnp
from jax import lax
from jax.experimental import pallas as pl
from jax.experimental.pallas import tpu as pltpu
from jax.sharding import PartitionSpec as P

IMG_PIX = 4096
EPS = 1e-06
DISTILL = 1.0

MESH = pl.DeviceIdType.MESH
HIGH = lax.Precision.HIGHEST
BF16 = jnp.bfloat16
F32 = jnp.float32

SIDE = 4
OTHERS = SIDE * SIDE - 1
TILE = (16, 128)
BANDS = 5
HEAD = 64
PARTS = 9
SHARE = 3
TILES = SIDE * SHARE + 1


def pack(slab0, slab1, last):
    band = [slice(16 * b, 16 * b + 16) for b in range(BANDS)]
    tiles = [slab0[at] for at in band] + [slab1[at] for at in band]
    tiles.append(last[band[0]] + pltpu.roll(last[band[1]], 64, 1))
    tiles.append(last[band[2]] + pltpu.roll(last[band[3]], 64, 1))
    return [t.astype(BF16) for t in tiles]


def pack_end(last, head):
    band = [slice(16 * b, 16 * b + 16) for b in range(BANDS)]
    end = last + head[band[0]]
    for b in range(1, BANDS):
        end = end + pltpu.roll(head[band[b]], PARTS * b, 1)
    return end.astype(BF16)


def unpack_last(ten, eleven, end):
    lane = lax.broadcasted_iota(jnp.int32, TILE, 1)
    values = [ten, pltpu.roll(ten, 64, 1), eleven, pltpu.roll(eleven, 64, 1), end]
    heads = [end] + [pltpu.roll(end, 128 - PARTS * b, 1) for b in range(1, BANDS)]
    return [jnp.where(lane < HEAD, v, h) for v, h in zip(values, heads)]


def dot(left, right, dims, **kw):
    return lax.dot_general(left, right, (dims, ((), ())), preferred_element_type=F32, **kw)


def kernel(
    loss_scale,
    x_hbm, table_hbm, w_in_hbm, w_down_hbm, levels_ref, w_rgb_ref, target_ref, counts_ref,
    pred_ref, sums_ref,
    x_ref, table_ref, w_in_ref, w_down_ref, in_sem,
    rgb_rows, rgb_parts, normed, wbuf, wext, wmat, head_t, hidden, slope, pred_mine, pred_other, g_rows, g_aug, g_aug_t, ends,
    gsend, gext, grecv, xrecv, zsend, zext, zrecv, fbuf,
    ax_send, ax_recv, ex_send, ex_recv, yx_send, yx_recv, bx_send, bx_recv, rx_send, rx_recv,
    a_send, a_recv, e_send, e_recv, y_send, y_recv, b_send, b_recv, p_send, p_recv,
    r_send, r_recv, z_send, z_recv, f_send, f_recv,
):
    pair = lax.axis_index("pair")
    dp = lax.axis_index("dp")
    fsdp = lax.axis_index("fsdp")
    x, zl = lax.div(dp, SIDE), lax.rem(dp, SIDE)
    y, zh = lax.div(fsdp, SIDE), lax.rem(fsdp, SIDE)
    xs, ys, zls, zhs = ([at] + [lax.rem(at + n, SIDE) for n in range(1, SIDE)] for at in (x, y, zl, zh))
    steps = (2, 1, 3, 0)
    around = [(a, b) for b in steps for a in steps if (a, b) != (0, 0)]
    here = y * SIDE + x
    channels, pixels = x_ref.shape
    rows = w_in_ref.shape[0]

    def device(x_, y_, zh_, zl_):
        return (pair, x_ * SIDE + zl_, y_ * SIDE + zh_)

    def plane_peer(a, b):
        return device(xs[a], ys[b], zh, zl)

    def dp_peer(a, b):
        return device(xs[a], y, zh, zls[b])

    def group_peer(k):
        return device(x, y, zhs[k], zl)

    barrier = pltpu.get_barrier_semaphore()

    def greet(peer):
        pl.semaphore_signal(barrier, inc=1, device_id=peer, device_id_type=MESH)

    for k in (1, 3):
        greet(group_peer(k))
    loads = {}
    for n, (src, dst) in enumerate(
        ((w_in_hbm, w_in_ref), (w_down_hbm, w_down_ref), (x_hbm, x_ref), (table_hbm, table_ref))
    ):
        loads[n] = pltpu.make_async_copy(src, dst, in_sem.at[n])
        loads[n].start()
    for a, b in around:
        greet(plane_peer(a, b))
    for b in (2, 1, 3):
        greet(dp_peer(0, b))
    greet((1 - pair, dp, fsdp))
    loads[0].wait()
    w_own = w_in_ref[...]
    last = w_own[:, 256:320].astype(F32)
    last = jnp.concatenate([last, jnp.zeros((rows, 64), F32)], axis=1)
    tiles = pack(w_own[:, 0:128], w_own[:, 128:256], last)
    for t in range(TILES - 1):
        wbuf[zh, y * SIDE + t // SHARE, t % SHARE] = tiles[t]

    rgb_rows[...] = jnp.zeros_like(rgb_rows)
    for copy in range(3):
        for k in range(3):
            at = 3 * copy + k
            rgb_rows[at : at + 1, :] = w_rgb_ref[k]
    part = rgb_rows[...]
    part_hi = part.astype(BF16).astype(F32)
    part_mid = (part - part_hi).astype(BF16).astype(F32)
    part_lo = part - part_hi - part_mid
    rgb_parts[...] = jnp.zeros_like(rgb_parts)
    for n, p in enumerate((part_hi, part_mid, part_lo)):
        rgb_parts[HEAD + 16 * n : HEAD + 16 * n + 16, :] = p.astype(BF16)
    loads[1].wait()
    head = dot(w_down_ref[...], rgb_parts[...], ((1,), (1,)))
    head = head + pltpu.roll(head, 112, 1) + pltpu.roll(head, 96, 1)
    lane = lax.broadcasted_iota(jnp.int32, (rows, 128), 1)
    head = jnp.where((lane >= HEAD) & (lane < HEAD + PARTS), head, 0.0)
    head_hi = head.astype(BF16).astype(F32)
    is_lo = (lane >= HEAD + 3) & (lane < HEAD + 6)
    head = jnp.where(is_lo, head - head_hi, head_hi)
    own_ext = wext.at[zh, y]
    own_ext[...] = pack_end(last[64:80], head)
    pl.semaphore_wait(barrier, OTHERS + 3 + 2 + 1)

    def remote(src, dst, send, recv, peer):
        return pltpu.make_async_remote_copy(
            src_ref=src, dst_ref=dst, send_sem=send, recv_sem=recv,
            device_id=peer, device_id_type=MESH,
        )

    def wait_bytes(ref, sem):
        pltpu.make_async_copy(ref, ref, sem).wait()

    quarter = wbuf.at[zh, here]
    along_z = {}
    for k in (1, 3):
        along_z[k] = remote(quarter, quarter, a_send.at[k], a_recv.at[k], group_peer(k))
        along_z[k].start()

    def when_mine(group, copy):
        @pl.when(x == group)
        def _():
            copy()

    block = wbuf.at[zh, pl.ds(y * SIDE, SIDE)]
    along_y = []
    for m in range(1, SIDE):
        c = remote(block, block, y_send.at[m], y_recv.at[m], plane_peer(0, m))
        c.start()
        along_y.append(c)

    along_z_ext = {}
    for k in (1, 3):
        along_z_ext[k] = remote(own_ext, own_ext, ax_send.at[k], ax_recv.at[k], group_peer(k))
        when_mine(zh, along_z_ext[k].start)
    for m in range(1, SIDE):
        c = remote(own_ext, own_ext, yx_send.at[m], yx_recv.at[m], plane_peer(0, m))
        c.start()
        along_y.append(c)

    loads[2].wait()
    loads[3].wait()
    image = ((dp * SIDE * SIDE + fsdp) * pixels) // IMG_PIX
    levels = levels_ref[...].astype(F32)
    spots = lax.broadcasted_iota(jnp.int32, levels.shape, 1)
    level = jnp.sum(jnp.where(spots == image, levels, 0.0), axis=1, keepdims=True)
    table_rows = lax.broadcasted_iota(jnp.int32, table_ref.shape, 0).astype(F32)
    gain = jnp.sum(jnp.where(table_rows == level, table_ref[...], 0.0), axis=0, keepdims=True)
    gain = jnp.concatenate([gain, jnp.zeros((1, 384 - channels), F32)], axis=1)
    gain = jnp.broadcast_to(gain, (128, 384)).T[:channels, 0:1]
    xf = x_ref[...].astype(F32)
    mean_sq = jnp.mean(xf * xf, axis=0, keepdims=True)
    whole = xf * lax.rsqrt(mean_sq + EPS) * gain
    whole = jnp.concatenate([whole, jnp.zeros((384 - channels, pixels), F32)], axis=0)
    normed[...] = whole.astype(BF16)

    row = lax.broadcasted_iota(jnp.int32, part.shape, 0)
    part = jnp.where(row < 3, part_hi, jnp.where(row < 6, part_mid, part_lo)).astype(BF16)
    direct = dot(part, x_ref[...], ((1,), (0,)))
    pred_mine[...] = jnp.zeros_like(pred_mine)
    pred_mine[0:3, :] = direct[0:3] + direct[3:6] + direct[6:9]

    wide = 512

    def assemble(group, yy):
        def tile(t):
            return wbuf[group, yy * SIDE + t // SHARE, t % SHARE]

        end = unpack_last(tile(10).astype(F32), tile(11).astype(F32), wext[group, yy].astype(F32))
        for band in range(BANDS):
            at = pl.ds(yy * rows + 16 * band, 16)
            wmat[group, at, 0:128] = tile(band)
            wmat[group, at, 128:256] = tile(BANDS + band)
            wmat[group, at, 256:384] = end[band].astype(BF16)

    def sigmoid(pre):
        return 0.5 * jnp.tanh(0.5 * pre) + 0.5

    def forward(group, now=True):
        def assemble_one(yy, carry):
            assemble(group, yy)
            return carry

        lax.fori_loop(0, SIDE, assemble_one, 0)
        head_t[group] = wmat[group, :, 256:384].astype(F32).T[HEAD : HEAD + 16].astype(BF16)

        def columns(n, carry):
            at = pl.ds(pl.multiple_of(n * wide, wide), wide)
            pre = dot(wmat[group], normed[:, at], ((1,), (0,)))
            sig = sigmoid(pre)
            act = pre * sig
            hid = act.astype(BF16)
            hidden[group, :, at] = hid
            slope[group, :, at] = sig + act * (1.0 - sig) if now else pre
            through = dot(head_t[group], hid, ((1,), (0,)))
            pred_mine[0:3, at] += through[0:3] + through[3:6]
            return carry

        lax.fori_loop(0, pixels // wide, columns, 0, unroll=True)

    relays = {}
    passed = wext.at[zhs[1], y]
    relay_ext = remote(passed, passed, ex_send, ex_recv, group_peer(3))

    def relay(k):
        group = zhs[-k]
        along_z[k].wait_recv()
        some = wbuf.at[group, here, pl.ds(0, 2) if k == 1 else pl.ds(2, 1)]
        relays[k] = remote(some, some, e_send.at[k], e_recv.at[k], group_peer(k))
        relays[k].start()

    def forward_on(k):
        group = zhs[-k]
        if k == 2:
            relays[1].wait_recv()
            relays[3].wait_recv()
        chunk = wbuf.at[group, here]
        extra = wext.at[group, y]

        for a, b in around:
            remote(chunk, chunk, b_send.at[k], b_recv.at[k], plane_peer(a, b)).start()

        @pl.when(x == group)
        def _():
            if k == 2:
                relay_ext.wait_recv()
            else:
                along_z_ext[k].wait_recv()
            if k == 3:
                relay_ext.start()
            for a, b in around:
                remote(extra, extra, bx_send.at[k], bx_recv.at[k], plane_peer(a, b)).start()

    far = zhs[2]
    def wait_group(k):
        group = zhs[-k]
        wait_bytes(wbuf.at[0, 0:OTHERS], b_recv.at[k])

        @pl.when(x == group)
        def _():
            wait_bytes(wext.at[0, 0 : SIDE - 1], bx_recv.at[k])

        @pl.when(x != group)
        def _():
            wait_bytes(wext.at[0], bx_recv.at[k])

    for k in (1, 3):
        relay(k)
        forward_on(k)
    for c in along_y:
        c.wait_recv()
    forward(zh)
    forward_on(2)
    samples = counts_ref[...].astype(F32)
    weight = samples / (samples + 64.0)
    g_rows[...] = jnp.zeros_like(g_rows)
    g_aug[...] = jnp.zeros_like(g_aug)
    for k in (1, 3):
        wait_group(k)
        forward(zhs[-k])
    wait_group(2)
    forward(far, now=False)

    swap = remote(pred_mine, pred_other, p_send, p_recv, (1 - pair, dp, fsdp))
    swap.start()
    pred = pred_mine[0:3, :]
    for k in range(3):
        pred_ref[k] = pred[k : k + 1]
    toward = weight * (pred - target_ref[...])

    def make_slope(n, carry):
        at = pl.ds(pl.multiple_of(n * wide, wide), wide)
        pre = slope[far, :, at]
        sig = sigmoid(pre)
        slope[far, :, at] = sig + pre * sig * (1.0 - sig)
        return carry

    lax.fori_loop(0, pixels // wide, make_slope, 0)
    swap.wait_recv()
    g_pred = (toward + DISTILL * (pred - pred_other[0:3, :])) * loss_scale
    g_hi = g_pred.astype(BF16).astype(F32)
    g_rows[0:3, :] = g_hi
    g_rows[3:6, :] = g_hi
    g_rows[6:9, :] = g_pred - g_hi
    g_aug[HEAD : HEAD + 16, :] = g_rows[...].astype(BF16)

    def backward_rows(group, picks):
        owners = [ys[b] for b in picks]

        def pick(ref, *rest):
            return jnp.concatenate([ref[(group, pl.ds(yy * rows, rows), *rest)] for yy in owners], axis=0)

        g_hidden = dot(pick(wmat, slice(256, 384)), g_aug[...], ((1,), (0,)))
        g_pre = (g_hidden * pick(slope, slice(None))).astype(BF16)
        grad = dot(g_pre, normed[...], ((1,), (1,)))
        for n, yy in enumerate(owners):
            at = slice(n * rows, n * rows + rows)
            tiles = pack(grad[at, 0:128], grad[at, 128:256], grad[at, 256:384])
            for t in range(TILES - 1):
                gsend[group, yy * SIDE + t // SHARE, t % SHARE] = tiles[t]
            ends[yy] = grad[n * rows + 64 : n * rows + 80, 256:384]

        for a, b in around:
            if b in picks:
                remote(
                    gsend.at[group, ys[b] * SIDE + xs[a]], grecv.at[group, here],
                    r_send.at[group], r_recv.at[group], plane_peer(a, b),
                ).start()

    def backward(group, parts, first):
        for picks in parts:
            backward_rows(group, picks)
        grecv[group, here] = gsend[group, here]

        if first:
            g_aug_t[...] = g_aug[...].astype(F32).T.astype(BF16)
        for_head = dot(hidden[group], g_aug_t[...], ((1,), (0,)))
        lane_g = lax.broadcasted_iota(jnp.int32, for_head.shape, 1)
        is_rest = (lane_g >= HEAD + 3) & (lane_g < HEAD + 6)
        for_head = jnp.where(is_rest, for_head - for_head.astype(BF16).astype(F32), for_head)
        for yy in range(SIDE):
            gext[group, yy] = pack_end(ends[yy], for_head[yy * rows : yy * rows + rows])

        def send_ext(b):
            remote(
                gext.at[group, ys[b]], xrecv.at[here], rx_send.at[group], rx_recv, device(group, ys[b], zh, zl)
            ).start()

        for b in (2, 1, 3):
            send_ext(b)

        @pl.when(x == group)
        def _():
            xrecv[here] = gext[group, y]

        @pl.when(x != group)
        def _():
            send_ext(0)

    order = [zhs[k] for k in steps]

    def plane_sum(group, own):
        wait_bytes(grecv.at[0, 0:OTHERS], r_recv.at[group])
        total = grecv[group, 0].astype(F32)
        for s in range(1, SIDE * SIDE):
            total = total + grecv[group, s].astype(F32)
        zsend[group] = total

        own_slot = zrecv.at[zh * SIDE + zl]

        for to in range(SHARE):
            piece = remote(zsend.at[group, to], own_slot, z_send, z_recv, device(x, y, group, to))
            if own:
                pl.when(to != zl)(piece.start)
            else:
                piece.start()

        @pl.when(x == group)
        def _():
            wait_bytes(xrecv.at[0:OTHERS], rx_recv)
            total = xrecv[0].astype(F32)
            for s in range(1, SIDE * SIDE):
                total = total + xrecv[s].astype(F32)
            zext[...] = total

            piece = remote(zext, own_slot, z_send, z_recv, device(x, y, group, SHARE))
            if own:
                pl.when(zl != SHARE)(piece.start)
            else:
                piece.start()

    for n, group in enumerate(order):
        backward(group, ((2, 1), (3, 0)) if n == 0 else ((2, 1, 3, 0),), n == 0)
    for k, group in zip(steps, order):
        plane_sum(group, k == 0)
    has_tile = (zl < SHARE) | (x == zh)

    @pl.when(zl < SHARE)
    def _():
        zrecv[zh * SIDE + zl] = zsend[zh, zl]

    @pl.when((zl == SHARE) & (x == zh))
    def _():
        zrecv[zh * SIDE + zl] = zext[...]

    @pl.when(has_tile)
    def _():
        wait_bytes(zrecv.at[0:OTHERS], z_recv)
        total = zrecv[0]
        for s in range(1, SIDE * SIDE):
            total = total + zrecv[s]
        own = jnp.where(zl < SHARE, x * SHARE + zl, TILES - 1)
        fbuf[own] = total

        for a, b in around:
            remote(fbuf.at[own], fbuf.at[own], f_send, f_recv, dp_peer(a, b)).start()

    for k in (1, 2, 3):
        group = zhs[-k]
        if k != 2:
            along_z[k].wait_send()
            when_mine(zh, along_z_ext[k].wait_send)
            relays[k].wait_send()
        wait_bytes(wbuf.at[0, 0:OTHERS], b_send.at[k])
        when_mine(group, lambda: wait_bytes(xrecv.at[0:OTHERS], bx_send.at[k]))
    when_mine(zhs[1], relay_ext.wait_send)
    for c in along_y:
        c.wait_send()
    swap.wait_send()
    for group in range(SIDE):
        wait_bytes(gsend.at[0, 0:OTHERS], r_send.at[group])

        @pl.when(x == group)
        def _():
            wait_bytes(gext.at[0, 0 : SIDE - 1], rx_send.at[group])

        @pl.when(x != group)
        def _():
            wait_bytes(gext.at[0], rx_send.at[group])

    @pl.when(has_tile)
    def _():
        wait_bytes(fbuf.at[0 : TILES - 1], z_send)
        wait_bytes(fbuf.at[0 : TILES - 1], f_recv)
        wait_bytes(zrecv.at[0:OTHERS], f_send)

    @pl.when(jnp.logical_not(has_tile))
    def _():
        wait_bytes(fbuf, z_send)
        wait_bytes(fbuf, f_recv)

    sums_ref[...] = fbuf[...]


def results(sums_ref, pred_in_ref, w_rgb_ref, pred_ref, grad_in_ref, grad_down_ref):
    pred_ref[...] = pred_in_ref[...]
    end = unpack_last(sums_ref[10], sums_ref[11], sums_ref[12])
    for band in range(BANDS):
        at = slice(16 * band, 16 * band + 16)
        grad_in_ref[at, 0:128] = sums_ref[band]
        grad_in_ref[at, 128:256] = sums_ref[BANDS + band]
        grad_in_ref[at, 256:320] = end[band][:, 0:64]
        total = 0.0
        for k in range(3):
            weight = sum(end[band][:, at + k : at + k + 1] for at in range(HEAD, HEAD + PARTS, 3))
            total = total + weight * w_rgb_ref[k]
        grad_down_ref[16 * band : 16 * band + 16, :] = total


def on_device(loss_scale, features, level_gain, levels, w_in, w_down, w_rgb, target, counts):
    channels, pixels = features.shape[1:]
    rows = w_in.shape[1]
    all_rows = SIDE * SIDE * rows
    group_rows = SIDE * rows
    plane = SIDE * SIDE
    dma = pltpu.SemaphoreType.DMA
    vmem = pl.BlockSpec(memory_space=pltpu.VMEM)
    flops = 2 * all_rows * pixels * (2 * 384 + 3 * 128)
    colours = jnp.transpose(w_rgb, (1, 0, 2))
    pred, sums = pl.pallas_call(
        lambda *refs: kernel(loss_scale, *refs),
        out_shape=(
            jax.ShapeDtypeStruct((3, 1, pixels), F32),
            jax.ShapeDtypeStruct((TILES, *TILE), F32),
        ),
        in_specs=[pl.BlockSpec(memory_space=pl.ANY)] * 4 + [vmem] * 4,
        out_specs=(vmem, vmem),
        scratch_shapes=[
            pltpu.VMEM((channels, pixels), BF16),
            pltpu.VMEM(level_gain.shape, F32),
            pltpu.VMEM((rows, channels), BF16),
            pltpu.VMEM((rows, channels), BF16),
            dma((4,)),
            pltpu.VMEM((16, channels), F32),
            pltpu.VMEM((128, channels), BF16),
            pltpu.VMEM((384, pixels), BF16),
            pltpu.VMEM((SIDE, plane, SHARE, *TILE), BF16),
            pltpu.VMEM((SIDE, SIDE, *TILE), BF16),
            pltpu.VMEM((SIDE, group_rows, 384), BF16),
            pltpu.VMEM((SIDE, 16, group_rows), BF16),
            pltpu.VMEM((SIDE, group_rows, pixels), BF16),
            pltpu.VMEM((SIDE, group_rows, pixels), F32),
            pltpu.VMEM((8, pixels), F32),
            pltpu.VMEM((8, pixels), F32),
            pltpu.VMEM((16, pixels), F32),
            pltpu.VMEM((128, pixels), BF16),
            pltpu.VMEM((pixels, 128), BF16),
            pltpu.VMEM((SIDE, *TILE), F32),
            pltpu.VMEM((SIDE, plane, SHARE, *TILE), BF16),
            pltpu.VMEM((SIDE, SIDE, *TILE), BF16),
            pltpu.VMEM((SIDE, plane, SHARE, *TILE), BF16),
            pltpu.VMEM((plane, *TILE), BF16),
            pltpu.VMEM((SIDE, SHARE, *TILE), F32),
            pltpu.VMEM(TILE, F32),
            pltpu.VMEM((plane, *TILE), F32),
            pltpu.VMEM((TILES, *TILE), F32),
            dma((SIDE,)), dma((SIDE,)), dma, dma, dma((SIDE,)), dma((SIDE,)), dma((SIDE,)), dma((SIDE,)), dma((SIDE,)), dma,
            dma((SIDE,)), dma((SIDE,)), dma((SIDE,)), dma((SIDE,)),
            dma((SIDE,)), dma((SIDE,)), dma((SIDE,)), dma((SIDE,)), dma, dma,
            dma((SIDE,)), dma((SIDE,)), dma, dma, dma, dma,
        ],
        compiler_params=pltpu.CompilerParams(
            collective_id=0, has_side_effects=True, vmem_limit_bytes=56 * 2**20
        ),
        cost_estimate=pl.CostEstimate(flops=flops, bytes_accessed=2**21, transcendentals=all_rows * pixels),
    )(features[0], level_gain, w_in[0], w_down[0], levels[None], colours, target, counts[None])
    pred, grad_in, grad_down = pl.pallas_call(
        results,
        out_shape=(
            jax.ShapeDtypeStruct((3, 1, pixels), F32),
            jax.ShapeDtypeStruct((rows, channels), F32),
            jax.ShapeDtypeStruct((rows, channels), F32),
        ),
        in_specs=[vmem] * 3,
        out_specs=(vmem, vmem, vmem),
    )(sums, pred, colours)
    return jnp.transpose(pred, (1, 0, 2)), grad_in[None], grad_down[None]


def solution(mesh):
    in_specs = (
        P("pair", None, ("dp", "fsdp")),
        P(),
        P(),
        P("pair", "fsdp", None),
        P("pair", "fsdp", None),
        P("pair", None, None),
        P(None, ("dp", "fsdp")),
        P(("dp", "fsdp")),
    )
    out_specs = (P("pair", None, ("dp", "fsdp")), P("pair", "fsdp", None), P("pair", "fsdp", None))

    def whole(features, *rest):
        loss_scale = math.sqrt(features.shape[1] / features.shape[2])
        return jax.shard_map(
            lambda *args: on_device(loss_scale, *args),
            mesh=mesh, in_specs=in_specs, out_specs=out_specs, check_vma=False,
        )(features, *rest)

    return whole
```

```python
import math

import jax
import jax.numpy as jnp
from jax import lax
from jax.experimental import pallas as pl
from jax.experimental.pallas import tpu as pltpu
from jax.sharding import PartitionSpec as P

IMG_PIX = 4096
EPS = 1e-06
DISTILL = 1.0

MESH = pl.DeviceIdType.MESH
HIGH = lax.Precision.HIGHEST
BF16 = jnp.bfloat16
F32 = jnp.float32

SIDE = 4
OTHERS = SIDE * SIDE - 1
TILE = (16, 128)
BANDS = 5
HEAD = 64
PARTS = 9
SHARE = 3
TILES = SIDE * SHARE + 1


def pack(slab0, slab1, last):
    band = [slice(16 * b, 16 * b + 16) for b in range(BANDS)]
    tiles = [slab0[at] for at in band] + [slab1[at] for at in band]
    tiles.append(last[band[0]] + pltpu.roll(last[band[1]], 64, 1))
    tiles.append(last[band[2]] + pltpu.roll(last[band[3]], 64, 1))
    return [t.astype(BF16) for t in tiles]


def pack_end(last, head):
    band = [slice(16 * b, 16 * b + 16) for b in range(BANDS)]
    end = last + head[band[0]]
    for b in range(1, BANDS):
        end = end + pltpu.roll(head[band[b]], PARTS * b, 1)
    return end.astype(BF16)


def unpack_last(ten, eleven, end):
    lane = lax.broadcasted_iota(jnp.int32, TILE, 1)
    values = [ten, pltpu.roll(ten, 64, 1), eleven, pltpu.roll(eleven, 64, 1), end]
    heads = [end] + [pltpu.roll(end, 128 - PARTS * b, 1) for b in range(1, BANDS)]
    return [jnp.where(lane < HEAD, v, h) for v, h in zip(values, heads)]


def dot(left, right, dims, **kw):
    return lax.dot_general(left, right, (dims, ((), ())), preferred_element_type=F32, **kw)


def kernel(
    loss_scale,
    x_hbm, table_hbm, w_in_hbm, w_down_hbm, levels_ref, w_rgb_ref, target_ref, counts_ref,
    pred_ref, sums_ref,
    x_ref, table_ref, w_in_ref, w_down_ref, in_sem,
    rgb_rows, rgb_parts, normed, wbuf, wext, wmat, head_t, hidden, slope, pred_mine, pred_other, g_rows, g_aug, g_aug_t, ends,
    gsend, gext, grecv, xrecv, zsend, zext, zrecv, fbuf,
    ax_send, ax_recv, ex_send, ex_recv, yx_send, yx_recv, bx_send, bx_recv, rx_send, rx_recv,
    a_send, a_recv, e_send, e_recv, y_send, y_recv, b_send, b_recv, p_send, p_recv,
    r_send, r_recv, z_send, z_recv, f_send, f_recv,
):
    pair = lax.axis_index("pair")
    dp = lax.axis_index("dp")
    fsdp = lax.axis_index("fsdp")
    x, zl = lax.div(dp, SIDE), lax.rem(dp, SIDE)
    y, zh = lax.div(fsdp, SIDE), lax.rem(fsdp, SIDE)
    xs, ys, zls, zhs = ([at] + [lax.rem(at + n, SIDE) for n in range(1, SIDE)] for at in (x, y, zl, zh))
    steps = (2, 1, 3, 0)
    around = [(a, b) for b in steps for a in steps if (a, b) != (0, 0)]
    here = y * SIDE + x
    channels, pixels = x_ref.shape
    rows = w_in_ref.shape[0]

    def device(x_, y_, zh_, zl_):
        return (pair, x_ * SIDE + zl_, y_ * SIDE + zh_)

    def plane_peer(a, b):
        return device(xs[a], ys[b], zh, zl)

    def dp_peer(a, b):
        return device(xs[a], y, zh, zls[b])

    def group_peer(k):
        return device(x, y, zhs[k], zl)

    barrier = pltpu.get_barrier_semaphore()

    def greet(peer):
        pl.semaphore_signal(barrier, inc=1, device_id=peer, device_id_type=MESH)

    for k in (1, 3):
        greet(group_peer(k))
    loads = {}
    for n, (src, dst) in enumerate(
        ((w_in_hbm, w_in_ref), (w_down_hbm, w_down_ref), (x_hbm, x_ref), (table_hbm, table_ref))
    ):
        loads[n] = pltpu.make_async_copy(src, dst, in_sem.at[n])
        loads[n].start()
    for a, b in around:
        greet(plane_peer(a, b))
    for b in (2, 1, 3):
        greet(dp_peer(0, b))
    greet((1 - pair, dp, fsdp))
    loads[0].wait()
    w_own = w_in_ref[...]
    last = w_own[:, 256:320].astype(F32)
    last = jnp.concatenate([last, jnp.zeros((rows, 64), F32)], axis=1)
    tiles = pack(w_own[:, 0:128], w_own[:, 128:256], last)
    for t in range(TILES - 1):
        wbuf[zh, y * SIDE + t // SHARE, t % SHARE] = tiles[t]

    rgb_rows[...] = jnp.zeros_like(rgb_rows)
    for copy in range(3):
        for k in range(3):
            at = 3 * copy + k
            rgb_rows[at : at + 1, :] = w_rgb_ref[k]
    part = rgb_rows[...]
    part_hi = part.astype(BF16).astype(F32)
    part_mid = (part - part_hi).astype(BF16).astype(F32)
    part_lo = part - part_hi - part_mid
    rgb_parts[...] = jnp.zeros_like(rgb_parts)
    for n, p in enumerate((part_hi, part_mid, part_lo)):
        rgb_parts[HEAD + 16 * n : HEAD + 16 * n + 16, :] = p.astype(BF16)
    loads[1].wait()
    head = dot(w_down_ref[...], rgb_parts[...], ((1,), (1,)))
    head = head + pltpu.roll(head, 112, 1) + pltpu.roll(head, 96, 1)
    lane = lax.broadcasted_iota(jnp.int32, (rows, 128), 1)
    head = jnp.where((lane >= HEAD) & (lane < HEAD + PARTS), head, 0.0)
    head_hi = head.astype(BF16).astype(F32)
    is_lo = (lane >= HEAD + 3) & (lane < HEAD + 6)
    head = jnp.where(is_lo, head - head_hi, head_hi)
    own_ext = wext.at[zh, y]
    own_ext[...] = pack_end(last[64:80], head)
    pl.semaphore_wait(barrier, OTHERS + 3 + 2 + 1)

    def remote(src, dst, send, recv, peer):
        return pltpu.make_async_remote_copy(
            src_ref=src, dst_ref=dst, send_sem=send, recv_sem=recv,
            device_id=peer, device_id_type=MESH,
        )

    def wait_bytes(ref, sem):
        pltpu.make_async_copy(ref, ref, sem).wait()

    quarter = wbuf.at[zh, here]
    along_z = {}
    for k in (1, 3):
        along_z[k] = remote(quarter, quarter, a_send.at[k], a_recv.at[k], group_peer(k))
        along_z[k].start()

    def when_mine(group, copy):
        @pl.when(x == group)
        def _():
            copy()

    block = wbuf.at[zh, pl.ds(y * SIDE, SIDE)]
    along_y = []
    for m in range(1, SIDE):
        c = remote(block, block, y_send.at[m], y_recv.at[m], plane_peer(0, m))
        c.start()
        along_y.append(c)

    along_z_ext = {}
    for k in (1, 3):
        along_z_ext[k] = remote(own_ext, own_ext, ax_send.at[k], ax_recv.at[k], group_peer(k))
        when_mine(zh, along_z_ext[k].start)
    for m in range(1, SIDE):
        c = remote(own_ext, own_ext, yx_send.at[m], yx_recv.at[m], plane_peer(0, m))
        c.start()
        along_y.append(c)

    loads[2].wait()
    loads[3].wait()
    image = ((dp * SIDE * SIDE + fsdp) * pixels) // IMG_PIX
    levels = levels_ref[...].astype(F32)
    spots = lax.broadcasted_iota(jnp.int32, levels.shape, 1)
    level = jnp.sum(jnp.where(spots == image, levels, 0.0), axis=1, keepdims=True)
    table_rows = lax.broadcasted_iota(jnp.int32, table_ref.shape, 0).astype(F32)
    gain = jnp.sum(jnp.where(table_rows == level, table_ref[...], 0.0), axis=0, keepdims=True)
    gain = jnp.concatenate([gain, jnp.zeros((1, 384 - channels), F32)], axis=1)
    gain = jnp.broadcast_to(gain, (128, 384)).T[:channels, 0:1]
    xf = x_ref[...].astype(F32)
    mean_sq = jnp.mean(xf * xf, axis=0, keepdims=True)
    whole = xf * lax.rsqrt(mean_sq + EPS) * gain
    whole = jnp.concatenate([whole, jnp.zeros((384 - channels, pixels), F32)], axis=0)
    normed[...] = whole.astype(BF16)

    row = lax.broadcasted_iota(jnp.int32, part.shape, 0)
    part = jnp.where(row < 3, part_hi, jnp.where(row < 6, part_mid, part_lo)).astype(BF16)
    direct = dot(part, x_ref[...], ((1,), (0,)))
    pred_mine[...] = jnp.zeros_like(pred_mine)
    pred_mine[0:3, :] = direct[0:3] + direct[3:6] + direct[6:9]

    wide = 1024

    def assemble(group, yy):
        def tile(t):
            return wbuf[group, yy * SIDE + t // SHARE, t % SHARE]

        end = unpack_last(tile(10).astype(F32), tile(11).astype(F32), wext[group, yy].astype(F32))
        for band in range(BANDS):
            at = pl.ds(yy * rows + 16 * band, 16)
            wmat[group, at, 0:128] = tile(band)
            wmat[group, at, 128:256] = tile(BANDS + band)
            wmat[group, at, 256:384] = end[band].astype(BF16)

    def sigmoid(pre):
        return 0.5 * jnp.tanh(0.5 * pre) + 0.5

    def forward(group, now=True):
        def assemble_one(yy, carry):
            assemble(group, yy)
            return carry

        lax.fori_loop(0, SIDE, assemble_one, 0)
        head_t[group] = wmat[group, :, 256:384].astype(F32).T[HEAD : HEAD + 16].astype(BF16)

        def columns(n, carry):
            at = pl.ds(pl.multiple_of(n * wide, wide), wide)
            pre = dot(wmat[group], normed[:, at], ((1,), (0,)))
            sig = sigmoid(pre)
            act = pre * sig
            hid = act.astype(BF16)
            hidden[group, :, at] = hid
            slope[group, :, at] = sig + act * (1.0 - sig) if now else pre
            through = dot(head_t[group], hid, ((1,), (0,)))
            pred_mine[0:3, at] += through[0:3] + through[3:6]
            return carry

        lax.fori_loop(0, pixels // wide, columns, 0, unroll=True)

    relays = {}
    passed = wext.at[zhs[1], y]
    relay_ext = remote(passed, passed, ex_send, ex_recv, group_peer(3))

    def relay(k):
        group = zhs[-k]
        along_z[k].wait_recv()
        some = wbuf.at[group, here, pl.ds(0, 2) if k == 1 else pl.ds(2, 1)]
        relays[k] = remote(some, some, e_send.at[k], e_recv.at[k], group_peer(k))
        relays[k].start()

    def forward_on(k):
        group = zhs[-k]
        if k == 2:
            relays[1].wait_recv()
            relays[3].wait_recv()
        chunk = wbuf.at[group, here]
        extra = wext.at[group, y]

        for a, b in around:
            remote(chunk, chunk, b_send.at[k], b_recv.at[k], plane_peer(a, b)).start()

        @pl.when(x == group)
        def _():
            if k == 2:
                relay_ext.wait_recv()
            else:
                along_z_ext[k].wait_recv()
            if k == 3:
                relay_ext.start()
            for a, b in around:
                remote(extra, extra, bx_send.at[k], bx_recv.at[k], plane_peer(a, b)).start()

    far = zhs[2]
    def wait_group(k):
        group = zhs[-k]
        wait_bytes(wbuf.at[0, 0:OTHERS], b_recv.at[k])

        @pl.when(x == group)
        def _():
            wait_bytes(wext.at[0, 0 : SIDE - 1], bx_recv.at[k])

        @pl.when(x != group)
        def _():
            wait_bytes(wext.at[0], bx_recv.at[k])

    for k in (1, 3):
        relay(k)
        forward_on(k)
    for c in along_y:
        c.wait_recv()
    forward(zh)
    forward_on(2)
    samples = counts_ref[...].astype(F32)
    weight = samples / (samples + 64.0)
    g_rows[...] = jnp.zeros_like(g_rows)
    g_aug[...] = jnp.zeros_like(g_aug)
    for k in (1, 3):
        wait_group(k)
        forward(zhs[-k])
    wait_group(2)
    forward(far, now=False)

    swap = remote(pred_mine, pred_other, p_send, p_recv, (1 - pair, dp, fsdp))
    swap.start()
    pred = pred_mine[0:3, :]
    for k in range(3):
        pred_ref[k] = pred[k : k + 1]
    toward = weight * (pred - target_ref[...])

    def make_slope(n, carry):
        at = pl.ds(pl.multiple_of(n * wide, wide), wide)
        pre = slope[far, :, at]
        sig = sigmoid(pre)
        slope[far, :, at] = sig + pre * sig * (1.0 - sig)
        return carry

    lax.fori_loop(0, pixels // wide, make_slope, 0)
    swap.wait_recv()
    g_pred = (toward + DISTILL * (pred - pred_other[0:3, :])) * loss_scale
    g_hi = g_pred.astype(BF16).astype(F32)
    g_rows[0:3, :] = g_hi
    g_rows[3:6, :] = g_hi
    g_rows[6:9, :] = g_pred - g_hi
    g_aug[HEAD : HEAD + 16, :] = g_rows[...].astype(BF16)

    def backward_rows(group, picks):
        owners = [ys[b] for b in picks]

        def pick(ref, *rest):
            return jnp.concatenate([ref[(group, pl.ds(yy * rows, rows), *rest)] for yy in owners], axis=0)

        g_hidden = dot(pick(wmat, slice(256, 384)), g_aug[...], ((1,), (0,)))
        g_pre = (g_hidden * pick(slope, slice(None))).astype(BF16)
        grad = dot(g_pre, normed[...], ((1,), (1,)))
        for n, yy in enumerate(owners):
            at = slice(n * rows, n * rows + rows)
            tiles = pack(grad[at, 0:128], grad[at, 128:256], grad[at, 256:384])
            for t in range(TILES - 1):
                gsend[group, yy * SIDE + t // SHARE, t % SHARE] = tiles[t]
            ends[yy] = grad[n * rows + 64 : n * rows + 80, 256:384]

        for a, b in around:
            if b in picks:
                remote(
                    gsend.at[group, ys[b] * SIDE + xs[a]], grecv.at[group, here],
                    r_send.at[group], r_recv.at[group], plane_peer(a, b),
                ).start()

    def backward(group, parts, first):
        for picks in parts:
            backward_rows(group, picks)
        grecv[group, here] = gsend[group, here]

        if first:
            g_aug_t[...] = g_aug[...].astype(F32).T.astype(BF16)
        for_head = dot(hidden[group], g_aug_t[...], ((1,), (0,)))
        lane_g = lax.broadcasted_iota(jnp.int32, for_head.shape, 1)
        is_rest = (lane_g >= HEAD + 3) & (lane_g < HEAD + 6)
        for_head = jnp.where(is_rest, for_head - for_head.astype(BF16).astype(F32), for_head)
        for yy in range(SIDE):
            gext[group, yy] = pack_end(ends[yy], for_head[yy * rows : yy * rows + rows])

        def send_ext(b):
            remote(
                gext.at[group, ys[b]], xrecv.at[here], rx_send.at[group], rx_recv, device(group, ys[b], zh, zl)
            ).start()

        for b in (2, 1, 3):
            send_ext(b)

        @pl.when(x == group)
        def _():
            xrecv[here] = gext[group, y]

        @pl.when(x != group)
        def _():
            send_ext(0)

    order = [zhs[k] for k in steps]

    def plane_sum(group, own):
        wait_bytes(grecv.at[0, 0:OTHERS], r_recv.at[group])
        total = grecv[group, 0].astype(F32)
        for s in range(1, SIDE * SIDE):
            total = total + grecv[group, s].astype(F32)
        zsend[group] = total

        own_slot = zrecv.at[zh * SIDE + zl]

        for to in range(SHARE):
            piece = remote(zsend.at[group, to], own_slot, z_send, z_recv, device(x, y, group, to))
            if own:
                pl.when(to != zl)(piece.start)
            else:
                piece.start()

        @pl.when(x == group)
        def _():
            wait_bytes(xrecv.at[0:OTHERS], rx_recv)
            total = xrecv[0].astype(F32)
            for s in range(1, SIDE * SIDE):
                total = total + xrecv[s].astype(F32)
            zext[...] = total

            piece = remote(zext, own_slot, z_send, z_recv, device(x, y, group, SHARE))
            if own:
                pl.when(zl != SHARE)(piece.start)
            else:
                piece.start()

    for n, group in enumerate(order):
        backward(group, ((2, 1, 3, 0),), n == 0)
    for k, group in zip(steps, order):
        plane_sum(group, k == 0)
    has_tile = (zl < SHARE) | (x == zh)

    @pl.when(zl < SHARE)
    def _():
        zrecv[zh * SIDE + zl] = zsend[zh, zl]

    @pl.when((zl == SHARE) & (x == zh))
    def _():
        zrecv[zh * SIDE + zl] = zext[...]

    @pl.when(has_tile)
    def _():
        wait_bytes(zrecv.at[0:OTHERS], z_recv)
        total = zrecv[0]
        for s in range(1, SIDE * SIDE):
            total = total + zrecv[s]
        own = jnp.where(zl < SHARE, x * SHARE + zl, TILES - 1)
        fbuf[own] = total

        for a, b in around:
            remote(fbuf.at[own], fbuf.at[own], f_send, f_recv, dp_peer(a, b)).start()

    for k in (1, 2, 3):
        group = zhs[-k]
        if k != 2:
            along_z[k].wait_send()
            when_mine(zh, along_z_ext[k].wait_send)
            relays[k].wait_send()
        wait_bytes(wbuf.at[0, 0:OTHERS], b_send.at[k])
        when_mine(group, lambda: wait_bytes(xrecv.at[0:OTHERS], bx_send.at[k]))
    when_mine(zhs[1], relay_ext.wait_send)
    for c in along_y:
        c.wait_send()
    swap.wait_send()
    for group in range(SIDE):
        wait_bytes(gsend.at[0, 0:OTHERS], r_send.at[group])

        @pl.when(x == group)
        def _():
            wait_bytes(gext.at[0, 0 : SIDE - 1], rx_send.at[group])

        @pl.when(x != group)
        def _():
            wait_bytes(gext.at[0], rx_send.at[group])

    @pl.when(has_tile)
    def _():
        wait_bytes(fbuf.at[0 : TILES - 1], z_send)
        wait_bytes(fbuf.at[0 : TILES - 1], f_recv)
        wait_bytes(zrecv.at[0:OTHERS], f_send)

    @pl.when(jnp.logical_not(has_tile))
    def _():
        wait_bytes(fbuf, z_send)
        wait_bytes(fbuf, f_recv)

    sums_ref[...] = fbuf[...]


def results(sums_ref, pred_in_ref, w_rgb_ref, pred_ref, grad_in_ref, grad_down_ref):
    pred_ref[...] = pred_in_ref[...]
    end = unpack_last(sums_ref[10], sums_ref[11], sums_ref[12])
    for band in range(BANDS):
        at = slice(16 * band, 16 * band + 16)
        grad_in_ref[at, 0:128] = sums_ref[band]
        grad_in_ref[at, 128:256] = sums_ref[BANDS + band]
        grad_in_ref[at, 256:320] = end[band][:, 0:64]
        total = 0.0
        for k in range(3):
            weight = sum(end[band][:, at + k : at + k + 1] for at in range(HEAD, HEAD + PARTS, 3))
            total = total + weight * w_rgb_ref[k]
        grad_down_ref[16 * band : 16 * band + 16, :] = total


def on_device(loss_scale, features, level_gain, levels, w_in, w_down, w_rgb, target, counts):
    channels, pixels = features.shape[1:]
    rows = w_in.shape[1]
    all_rows = SIDE * SIDE * rows
    group_rows = SIDE * rows
    plane = SIDE * SIDE
    dma = pltpu.SemaphoreType.DMA
    vmem = pl.BlockSpec(memory_space=pltpu.VMEM)
    flops = 2 * all_rows * pixels * (2 * 384 + 3 * 128)
    colours = jnp.transpose(w_rgb, (1, 0, 2))
    pred, sums = pl.pallas_call(
        lambda *refs: kernel(loss_scale, *refs),
        out_shape=(
            jax.ShapeDtypeStruct((3, 1, pixels), F32),
            jax.ShapeDtypeStruct((TILES, *TILE), F32),
        ),
        in_specs=[pl.BlockSpec(memory_space=pl.ANY)] * 4 + [vmem] * 4,
        out_specs=(vmem, vmem),
        scratch_shapes=[
            pltpu.VMEM((channels, pixels), BF16),
            pltpu.VMEM(level_gain.shape, F32),
            pltpu.VMEM((rows, channels), BF16),
            pltpu.VMEM((rows, channels), BF16),
            dma((4,)),
            pltpu.VMEM((16, channels), F32),
            pltpu.VMEM((128, channels), BF16),
            pltpu.VMEM((384, pixels), BF16),
            pltpu.VMEM((SIDE, plane, SHARE, *TILE), BF16),
            pltpu.VMEM((SIDE, SIDE, *TILE), BF16),
            pltpu.VMEM((SIDE, group_rows, 384), BF16),
            pltpu.VMEM((SIDE, 16, group_rows), BF16),
            pltpu.VMEM((SIDE, group_rows, pixels), BF16),
            pltpu.VMEM((SIDE, group_rows, pixels), F32),
            pltpu.VMEM((8, pixels), F32),
            pltpu.VMEM((8, pixels), F32),
            pltpu.VMEM((16, pixels), F32),
            pltpu.VMEM((128, pixels), BF16),
            pltpu.VMEM((pixels, 128), BF16),
            pltpu.VMEM((SIDE, *TILE), F32),
            pltpu.VMEM((SIDE, plane, SHARE, *TILE), BF16),
            pltpu.VMEM((SIDE, SIDE, *TILE), BF16),
            pltpu.VMEM((SIDE, plane, SHARE, *TILE), BF16),
            pltpu.VMEM((plane, *TILE), BF16),
            pltpu.VMEM((SIDE, SHARE, *TILE), F32),
            pltpu.VMEM(TILE, F32),
            pltpu.VMEM((plane, *TILE), F32),
            pltpu.VMEM((TILES, *TILE), F32),
            dma((SIDE,)), dma((SIDE,)), dma, dma, dma((SIDE,)), dma((SIDE,)), dma((SIDE,)), dma((SIDE,)), dma((SIDE,)), dma,
            dma((SIDE,)), dma((SIDE,)), dma((SIDE,)), dma((SIDE,)),
            dma((SIDE,)), dma((SIDE,)), dma((SIDE,)), dma((SIDE,)), dma, dma,
            dma((SIDE,)), dma((SIDE,)), dma, dma, dma, dma,
        ],
        compiler_params=pltpu.CompilerParams(
            collective_id=0, has_side_effects=True, vmem_limit_bytes=56 * 2**20
        ),
        cost_estimate=pl.CostEstimate(flops=flops, bytes_accessed=2**21, transcendentals=all_rows * pixels),
    )(features[0], level_gain, w_in[0], w_down[0], levels[None], colours, target, counts[None])
    pred, grad_in, grad_down = pl.pallas_call(
        results,
        out_shape=(
            jax.ShapeDtypeStruct((3, 1, pixels), F32),
            jax.ShapeDtypeStruct((rows, channels), F32),
            jax.ShapeDtypeStruct((rows, channels), F32),
        ),
        in_specs=[vmem] * 3,
        out_specs=(vmem, vmem, vmem),
    )(sums, pred, colours)
    return jnp.transpose(pred, (1, 0, 2)), grad_in[None], grad_down[None]


def solution(mesh):
    in_specs = (
        P("pair", None, ("dp", "fsdp")),
        P(),
        P(),
        P("pair", "fsdp", None),
        P("pair", "fsdp", None),
        P("pair", None, None),
        P(None, ("dp", "fsdp")),
        P(("dp", "fsdp")),
    )
    out_specs = (P("pair", None, ("dp", "fsdp")), P("pair", "fsdp", None), P("pair", "fsdp", None))

    def whole(features, *rest):
        loss_scale = math.sqrt(features.shape[1] / features.shape[2])
        return jax.shard_map(
            lambda *args: on_device(loss_scale, *args),
            mesh=mesh, in_specs=in_specs, out_specs=out_specs, check_vma=False,
        )(features, *rest)

    return whole
```
